512 devices in a mesh: seq: 32 (over x, y), head: 16 (over z, core).
Axes of the slice: x: 4, y: 8, z: 8, core: 2. Of those that a mesh axis runs over, the one named last changes fastest.
Arguments:
- qkv_raw: bfloat16 [16384, 3, 4096], P('seq', None, 'head'), may hold values from -6 to 6
- conv_weight: float32 [3, 4, 4096], P(None, None, 'head'), may hold values from -3 to 3
- norm_gain: float32 [4096], P('head'), may hold values from 0.1 to 1.9
- doc_starts: int32 [4], replicated, may hold values from 0 to 15744, as said below
- cotangent: bfloat16 [16384, 4096], P('seq', 'head'), may hold values from -6 to 6
Outputs:
- attn_out: bfloat16 [16384, 4096], P(('seq', 'head'))
- grad_input: bfloat16 [16384, 3, 4096], P(('seq', 'head'))
The draws below stay inside these ranges and needn't reach their ends.
Inputs may be any that keep to these rules, and one draw needn't show every extreme that they name: `doc_starts`: the first entry is 0 and the last is 15744; the entries rise strictly and each is a multiple of 128.
All inputs are finite; a program needn't handle non-finite values.
Results may differ from the reference program's by a relative error of at most 0.0062.
Values may be sent and summed in bfloat16 or wider, within the bound.
No kernel may reach another device: no remote copies, remote signals or barrier semaphores. Data moves between devices by JAX's collectives and lax.ppermute only.
A program may use at most 64 MiB of HBM per device.

```python
from functools import partial
import jax
import jax.numpy as jnp
from jax import lax

HEADS = 32
HEAD_DIM = 128
D = 4096
TAPS = 4
TOK_SEQ = 512
DOCS = 4
TOKENS = 16384


def draw_doc_starts(key, part):
    key = jax.random.fold_in(key, 7)
    last_granule = (TOKENS - TOK_SEQ) // 128 - 1
    shuffled = jax.random.permutation(key, last_granule - 1) + 1
    picked = jnp.sort(shuffled[:DOCS - 2]).astype(jnp.int32)
    ends = jnp.concatenate([jnp.zeros((1,), jnp.int32), picked, jnp.full((1,), last_granule, jnp.int32)])
    return (ends * 128).astype(jnp.int32)


def block_levels(stream_key, shape, split, least, largest):
    factor_of, own = 1.0, jax.random.fold_in(stream_key, 6)
    for axis_at, parts in split:
        steps = jnp.exp(jax.random.uniform(jax.random.fold_in(own, axis_at), (parts,), jnp.float32, least / len(split), largest / len(split)))
        factor_of = factor_of * jnp.repeat(steps, shape[axis_at] // parts).reshape([-1 if axis == axis_at else 1 for axis in range(len(shape))])
    return factor_of


def centred(own_key, dims, deviation, limit, pieces=(), kind=jnp.bfloat16):
    drawn = jax.random.normal(own_key, dims, jnp.float32) * deviation
    if len(pieces) > 0:
        drawn = block_levels(own_key, dims, pieces, -0.22, 0.18) * drawn
    return jnp.clip(drawn, min=-limit, max=limit).astype(kind)


def setup_inputs(seed: int = 0) -> dict:
    key_of = jax.random.split(jax.random.key(seed), 6)
    qkv_raw = centred(key_of[0], (TOKENS, 3, D), 1.0, 6.0, ((0, 32), (2, 16)))
    conv_weight = centred(key_of[1], (3, TAPS, D), 0.5, 3.0, ((2, 16),), jnp.float32)
    norm_gain = jnp.clip(1.0 + 0.18 * jax.random.normal(key_of[2], (D,), jnp.float32), 0.1, 1.9)
    doc_starts = draw_doc_starts(jax.random.fold_in(key_of[5], 71), 0)
    cotangent = centred(key_of[4], (TOKENS, D), 1.0, 6.0, ((0, 32), (1, 16)))
    return {"qkv_raw": qkv_raw, "conv_weight": conv_weight, "norm_gain": norm_gain, "doc_starts": doc_starts, "cotangent": cotangent}


highest = lax.Precision.HIGHEST

def segment_ids(doc_starts, positions):
    return lax.optimization_barrier(jnp.sum((doc_starts[None, :] <= positions[:, None]).astype(jnp.int32), axis=1)) - 1

def silu_slope(inputs):
    sigma = jax.nn.sigmoid(inputs)
    return sigma * (1.0 + inputs * (1.0 - sigma))

def causal_conv(raw_rows, taps, segments):
    total = taps[:, 0, :] * raw_rows
    for offset in range(1, TAPS):
        lagged = jnp.concatenate([jnp.zeros((offset,) + raw_rows.shape[1:], jnp.float32), raw_rows[:-offset]], axis=0)
        same_doc = jnp.concatenate([jnp.zeros((offset,), jnp.bool_), segments[offset:] == segments[:-offset]])
        total = total + jnp.where(same_doc[:, None, None], taps[:, offset, :] * lagged, 0.0)
    return total

def conv_transpose(grad_rows, taps, segments):
    total = taps[:, 0, :] * grad_rows
    for offset in range(1, TAPS):
        leading = jnp.concatenate([grad_rows[offset:], jnp.zeros((offset,) + grad_rows.shape[1:], jnp.float32)], axis=0)
        same_doc = jnp.concatenate([segments[:-offset] == segments[offset:], jnp.zeros((offset,), jnp.bool_)])
        total = total + jnp.where(same_doc[:, None, None], taps[:, offset, :] * leading, 0.0)
    return total

def head_pass(segments, packed):
    raw_rows, taps, gain_row, cot_rows = packed
    conv = causal_conv(raw_rows.astype(jnp.float32), taps, segments)
    queries = jax.nn.silu(conv[:, 0]).astype(jnp.bfloat16)
    key_rows = jax.nn.silu(conv[:, 1]).astype(jnp.bfloat16)
    values = conv[:, 2].astype(jnp.bfloat16)
    length = segments.shape[0]
    block_len = min(512, length)
    blocks = length // block_len

    def to_blocks(tensor):
        return tensor.reshape((blocks, block_len) + tensor.shape[1:])
    causal = jnp.arange(block_len)[:, None] >= jnp.arange(block_len)[None, :]
    seg_blocks = to_blocks(segments)

    def forward_block(loop_carry, inputs):
        carried_state, prev_seg = loop_carry
        block_q, block_k, block_v, block_seg = inputs
        doc_mask = causal & (block_seg[:, None] == block_seg[None, :])
        scores = jnp.where(doc_mask, jnp.dot(block_q, block_k.T, preferred_element_type=jnp.float32), 0.0)
        local_part = jnp.dot(scores, block_v.astype(jnp.float32), precision=highest)
        carried = jnp.where((block_seg == prev_seg)[:, None], jnp.dot(block_q.astype(jnp.float32), carried_state, precision=highest), 0.0)
        last_seg = block_seg[-1].astype(jnp.int32)
        masked_k = jnp.where((block_seg == last_seg)[:, None], block_k, jnp.zeros_like(block_k))
        summary = jnp.dot(masked_k.T, block_v, preferred_element_type=jnp.float32)
        new_state = (summary + jnp.where(last_seg == prev_seg, carried_state, 0.0)).astype(jnp.float32)
        return ((new_state, last_seg), (local_part + carried, carried_state))
    start_carry = (jnp.zeros((HEAD_DIM, HEAD_DIM), jnp.float32), jnp.array(-1, jnp.int32))
    unused_carry, (attn_blocks, states_in) = lax.scan(forward_block, start_carry, (to_blocks(queries), to_blocks(key_rows), to_blocks(values), seg_blocks))
    attn = attn_blocks.reshape(length, HEAD_DIM)
    msq = lax.optimization_barrier(jnp.mean(attn * attn, axis=-1, keepdims=True))
    bound = msq > 1.0
    scale = lax.rsqrt(jnp.maximum(msq, 1.0))
    attn_out = (attn * scale * gain_row).astype(jnp.bfloat16)
    scaled_cot = cot_rows.astype(jnp.float32) * gain_row
    inner = lax.optimization_barrier(jnp.mean(scaled_cot * attn, axis=-1, keepdims=True))
    grad_norm = (scale * scaled_cot - jnp.where(bound, attn * scale * scale * scale * inner, 0.0)).astype(jnp.bfloat16)
    prev_segs = jnp.concatenate([jnp.array([-1], jnp.int32), seg_blocks[:-1, -1].astype(jnp.int32)])

    def backward_block(loop_carry, inputs):
        future, next_seg = loop_carry
        block_q, block_k, block_v, block_g, block_seg, state_in, prev_seg = inputs
        doc_mask = causal & (block_seg[:, None] == block_seg[None, :])
        scores = jnp.where(doc_mask, jnp.dot(block_q, block_k.T, preferred_element_type=jnp.float32), 0.0)
        grad_scores = jnp.where(doc_mask, jnp.dot(block_g, block_v.T, preferred_element_type=jnp.float32), 0.0)
        q_float = block_q.astype(jnp.float32)
        k_float = block_k.astype(jnp.float32)
        v_float = block_v.astype(jnp.float32)
        g_float = block_g.astype(jnp.float32)
        grad_q = jnp.dot(grad_scores, k_float, precision=highest) + jnp.where((block_seg == prev_seg)[:, None], jnp.dot(g_float, state_in.T, precision=highest), 0.0)
        apply_next = (block_seg == next_seg)[:, None]
        grad_k = jnp.dot(grad_scores.T, q_float, precision=highest) + jnp.where(apply_next, jnp.dot(v_float, future.T, precision=highest), 0.0)
        grad_v = jnp.dot(scores.T, g_float, precision=highest) + jnp.where(apply_next, jnp.dot(k_float, future, precision=highest), 0.0)
        first_seg = block_seg[0].astype(jnp.int32)
        masked_q = jnp.where((block_seg == first_seg)[:, None], block_q, jnp.zeros_like(block_q))
        summary = jnp.dot(masked_q.T, block_g, preferred_element_type=jnp.float32)
        new_future = (summary + jnp.where(first_seg == next_seg, future, 0.0)).astype(jnp.float32)
        return ((new_future, first_seg), (grad_q, grad_k, grad_v))
    unused_back, (grad_q, grad_k, grad_v) = lax.scan(backward_block, start_carry, (to_blocks(queries), to_blocks(key_rows), to_blocks(values), to_blocks(grad_norm), seg_blocks, states_in, prev_segs), reverse=True)
    grad_conv = jnp.stack([grad_q.reshape(length, HEAD_DIM) * silu_slope(conv[:, 0]), grad_k.reshape(length, HEAD_DIM) * silu_slope(conv[:, 1]), grad_v.reshape(length, HEAD_DIM)], axis=1)
    grad_input = conv_transpose(grad_conv, taps, segments).astype(jnp.bfloat16)
    return (attn_out, grad_input)

def reference(qkv_raw, conv_weight, norm_gain, doc_starts, cotangent):
    length = qkv_raw.shape[0]
    segments = segment_ids(doc_starts, jnp.arange(length, dtype=jnp.int32))
    per_head = (qkv_raw.reshape(length, 3, HEADS, HEAD_DIM).transpose(2, 0, 1, 3), conv_weight.reshape(3, TAPS, HEADS, HEAD_DIM).transpose(2, 0, 1, 3), norm_gain.reshape(HEADS, HEAD_DIM), cotangent.reshape(length, HEADS, HEAD_DIM).transpose(1, 0, 2))
    out_heads, grad_heads = lax.map(partial(head_pass, segments), per_head)
    attn_out = out_heads.transpose(1, 0, 2).reshape(length, HEADS * HEAD_DIM)
    grad_input = grad_heads.transpose(1, 2, 0, 3).reshape(length, 3, HEADS * HEAD_DIM)
    return (attn_out, grad_input)
```

```python
import jax
import jax.numpy as jnp
from jax import lax
from jax.experimental import pallas as pl
from jax.experimental.pallas import tpu as pltpu
from jax.sharding import PartitionSpec as P

HEAD_DIM = 128
TAPS = 4
CHUNK = 128
HALO = 16
FAR = 1 << 30

f32 = jnp.float32
bf16 = jnp.bfloat16


def nt(a, b):
    return lax.dot_general(a, b, (((1,), (1,)), ((), ())), preferred_element_type=f32)


def nn(a, b):
    return lax.dot_general(a, b, (((1,), (0,)), ((), ())), preferred_element_type=f32)


def tn(a, b):
    return lax.dot_general(a, b, (((0,), (0,)), ((), ())), preferred_element_type=f32)


def doc_start(starts, first, pos):
    found = jnp.int32(-FAR)
    for d in range(starts.shape[0]):
        rel = starts[d] - first
        found = jnp.maximum(found, jnp.where(rel <= pos, rel, -FAR))
    return found


def doc_end(starts, first, pos):
    found = jnp.int32(FAR)
    for d in range(starts.shape[0]):
        rel = starts[d] - first
        found = jnp.minimum(found, jnp.where(rel > pos, rel, FAR))
    return found


def row_starts(starts, first, rows):
    found = jnp.full(rows.shape, -FAR, jnp.int32)
    for d in range(starts.shape[0]):
        rel = starts[d] - first
        found = jnp.maximum(found, jnp.where(rows >= rel, rel, -FAR))
    return found


def iota(shape, axis, base=0):
    return lax.broadcasted_iota(jnp.int32, shape, axis) + base


def conv_kernel(starts, raw, rim, halo, taps, qkv, slope, summary):
    rows = raw.shape[1]
    first = lax.axis_index("seq") * rows
    total = HALO + rows + HALO
    place = iota((total, HEAD_DIM), 0, -HALO)
    age = place - row_starts(starts, first, place)
    made = []
    for m in range(3):
        ext = jnp.concatenate([rim[m], raw[m], halo[m]], axis=0).astype(f32)
        conv = taps[m, 0:1] * ext
        for j in range(1, TAPS):
            conv = conv + jnp.where(age >= j, taps[m, j : j + 1] * pltpu.roll(ext, j, 0), 0.0)
        conv = conv[HALO:]
        if m < 2:
            sigma = 1.0 / (1.0 + jnp.exp(-conv))
            slope[m] = sigma * (1.0 + conv * (1.0 - sigma))
            conv = conv * sigma
        made.append(conv.astype(bf16))
        qkv[m] = made[m]
    last = doc_start(starts, first, rows - 1)
    keep = iota((rows, HEAD_DIM), 0) >= last
    masked_k = jnp.where(keep, made[1][:rows], jnp.zeros((), bf16))
    summary[...] = tn(masked_k, made[2][:rows])


def local_kernel(starts, qkv, local):
    total = qkv.shape[1]
    rows = total - HALO
    first = lax.axis_index("seq") * rows
    for low in range(0, total, CHUNK):
        high = min(low + CHUNK, total)
        size = high - low
        start = doc_start(starts, first, low)
        scores = nt(qkv[0, low:high], qkv[1, :high])
        t, s = iota((size, high), 0, low), iota((size, high), 1)
        scores = jnp.where((s <= t) & (s >= start), scores, 0.0).astype(bf16)
        local[low:high] = nn(scores, qkv[2, :high])


def norm_kernel(starts, qkv, local, incoming, cot, halo, gain, attn_out, grad_norm, back):
    total = local.shape[0]
    rows = total - HALO
    first = lax.axis_index("seq") * rows
    place = iota((total, HEAD_DIM), 0)
    prev = row_starts(starts, first, place) < 0
    q = qkv[0]
    attn = local[...] + jnp.where(prev, nn(q, incoming[...].astype(bf16)), 0.0)
    msq = jnp.mean(attn * attn, axis=-1, keepdims=True)
    scale = lax.rsqrt(jnp.maximum(msq, 1.0))
    gains = gain[...]
    attn_out[...] = (attn[:rows] * scale[:rows] * gains).astype(bf16)
    scaled = jnp.concatenate([cot[...], halo[0]], axis=0).astype(f32) * gains
    inner = jnp.mean(scaled * attn, axis=-1, keepdims=True)
    factor = jnp.where(msq > 1.0, scale * scale * scale * inner, 0.0)
    grad = (scale * scaled - attn * factor).astype(bf16)
    grad_norm[...] = grad
    masked_q = jnp.where(prev[:rows], q[:rows], jnp.zeros((), bf16))
    back[...] = tn(masked_q, grad[:rows])


def conv_back(grad, taps, m, age, rows):
    total = grad.shape[0]
    out = taps[m, 0:1] * grad[:rows]
    for j in range(1, TAPS):
        term = jnp.where(age >= j, taps[m, j : j + 1] * grad, 0.0)
        out = out + pltpu.roll(term, total - j, 0)[:rows]
    return out.astype(bf16)


def grad_kernel(starts, qkv, grad_norm, slope, incoming, taps, attn_out, early, local_k, local_v):
    total = grad_norm.shape[0]
    rows = total - HALO
    first = lax.axis_index("seq") * rows
    place = iota((total, HEAD_DIM), 0)
    begin = row_starts(starts, first, place)
    carried = jnp.where(begin < 0, nt(grad_norm[...], incoming[...].astype(bf16)), 0.0)
    parts = []
    for low in range(0, total, CHUNK):
        high = min(low + CHUNK, total)
        size = high - low
        start = doc_start(starts, first, low)
        scores = nt(grad_norm[low:high], qkv[2, :high])
        t, s = iota((size, high), 0, low), iota((size, high), 1)
        scores = jnp.where((s <= t) & (s >= start), scores, 0.0).astype(bf16)
        parts.append(nn(scores, qkv[1, :high]))
    grad_q = (jnp.concatenate(parts, axis=0) + carried) * slope[0]
    out = conv_back(grad_q, taps, 0, place - begin, rows)
    early[:, 0] = attn_out[...].reshape(early.shape[0], early.shape[2], HEAD_DIM)
    early[:, 1] = out.reshape(early.shape[0], early.shape[2], HEAD_DIM)
    for low in range(0, rows, CHUNK):
        high = low + CHUNK
        end = doc_end(starts, first, low)
        s, t = iota((CHUNK, rows - low), 0, low), iota((CHUNK, rows - low), 1, low)
        keep = (t >= s) & (t < end)
        scores = jnp.where(keep, nt(qkv[2, low:high], grad_norm[low:rows]), 0.0).astype(bf16)
        local_k[low:high] = nn(scores, qkv[0, low:rows])
        scores = jnp.where(keep, nt(qkv[1, low:high], qkv[0, low:rows]), 0.0).astype(bf16)
        local_v[low:high] = nn(scores, grad_norm[low:rows])
    s, t = iota((HALO, HALO), 0), iota((HALO, HALO), 1)
    scores = jnp.where(t < s, -nt(qkv[2, rows:], grad_norm[rows:]), 0.0).astype(bf16)
    local_k[rows:] = nn(scores, qkv[0, rows:])
    scores = jnp.where(t < s, -nt(qkv[1, rows:], qkv[0, rows:]), 0.0).astype(bf16)
    local_v[rows:] = nn(scores, grad_norm[rows:])


def last_kernel(starts, qkv, slope, local_k, local_v, future, taps, late):
    total = local_k.shape[0]
    rows = total - HALO
    first = lax.axis_index("seq") * rows
    place = iota((total, HEAD_DIM), 0)
    age = place - row_starts(starts, first, place)
    after = place >= doc_start(starts, first, rows)
    state = future[...].astype(bf16)
    grad_k = (local_k[...] + jnp.where(after, nt(qkv[2], state), 0.0)) * slope[0]
    grad_v = local_v[...] + jnp.where(after, nn(qkv[1], state), 0.0)
    shape = (late.shape[0], late.shape[2], HEAD_DIM)
    late[:, 0] = conv_back(grad_k, taps, 1, age, rows).reshape(shape)
    late[:, 1] = conv_back(grad_v, taps, 2, age, rows).reshape(shape)


def scan_kernel(reverse, rows, starts, sums, out):
    count = sums.shape[0]
    state = jnp.zeros(sums.shape[1:], f32)
    order = range(count - 1, -1, -1) if reverse else range(count)
    for i in order:
        out[i] = state
        open_here = jnp.bool_(True)
        for d in range(starts.shape[0]):
            here = (starts[d] >= i * rows) & (starts[d] < (i + 1) * rows)
            open_here = open_here & jnp.logical_not(here)
        state = sums[i] + jnp.where(open_here, state, 0.0)


def gather_kernel(early, late, out, grad):
    count, _, _, width = early.shape
    for i in range(count):
        columns = slice(i * width, (i + 1) * width)
        out[:, columns] = early[i, 0]
        grad[0, :, columns] = early[i, 1]
        grad[1, :, columns] = late[i, 0]
        grad[2, :, columns] = late[i, 1]


def shards(qkv_raw, conv_weight, norm_gain, doc_starts, cotangent):
    rows = qkv_raw.shape[0]
    width = qkv_raw.shape[2]
    heads = width // HEAD_DIM
    total = rows + HALO
    devices = lax.axis_size("seq")
    columns = lax.axis_size("head")
    piece = rows // columns
    raw = qkv_raw.transpose(1, 0, 2)
    gain = norm_gain.reshape(1, width)

    ahead = [(i, i + 1) for i in range(devices - 1)]
    behind = [(i + 1, i) for i in range(devices - 1)]
    rim = lax.ppermute(raw[:, rows - HALO :], "seq", ahead)
    halo = lax.ppermute(
        jnp.concatenate([raw[:, :HALO], cotangent[None, :HALO]], axis=0), "seq", behind
    )

    smem = pl.BlockSpec(memory_space=pltpu.SMEM)

    def per_head(shape, axis):
        return pl.BlockSpec(shape, lambda h: tuple(h if a == axis else 0 for a in range(len(shape))))

    def call(body, ins, outs, *args, grid=(heads,)):
        return pl.pallas_call(
            body,
            grid=grid,
            in_specs=[smem] + ins,
            out_specs=[spec for spec, _ in outs],
            out_shape=[shape for _, shape in outs],
            compiler_params=pltpu.CompilerParams(vmem_limit_bytes=48 * 1024 * 1024),
        )(doc_starts, *args)

    def whole(dims, kind):
        return jax.ShapeDtypeStruct(dims, kind)

    hd = HEAD_DIM
    spec_qkv = per_head((3, total, hd), 2)
    spec_taps = per_head((3, TAPS, hd), 2)
    spec_total = per_head((total, hd), 1)
    spec_rows = per_head((rows, hd), 1)
    spec_state = per_head((hd, hd), 0)
    shape_state = whole((heads * hd, hd), f32)

    qkv, slope, summary = call(
        conv_kernel,
        [per_head((3, rows, hd), 2), per_head((3, HALO, hd), 2), per_head((4, HALO, hd), 2), spec_taps],
        [
            (spec_qkv, whole((3, total, width), bf16)),
            (per_head((2, total, hd), 2), whole((2, total, width), f32)),
            (spec_state, shape_state),
        ],
        raw, rim, halo, conv_weight,
    )
    (local,) = call(
        local_kernel, [spec_qkv], [(spec_total, whole((total, width), f32))], qkv
    )

    def scan(sums, reverse):
        share = sums.reshape(devices, -1, hd)
        share = lax.all_to_all(share, "seq", 0, 0, tiled=True)
        flat = pl.BlockSpec(share.shape, lambda: (0, 0, 0))
        (share,) = call(
            lambda *refs: scan_kernel(reverse, rows, *refs),
            [flat], [(flat, whole(share.shape, f32))], share, grid=(),
        )
        return lax.all_to_all(share, "seq", 0, 0, tiled=True).reshape(sums.shape)

    incoming = scan(summary, False)
    attn_out, grad_norm, back = call(
        norm_kernel,
        [
            spec_qkv, spec_total, spec_state, spec_rows,
            pl.BlockSpec((1, HALO, hd), lambda h: (3, 0, h)), per_head((1, hd), 1),
        ],
        [
            (spec_rows, whole((rows, width), bf16)),
            (spec_total, whole((total, width), bf16)),
            (spec_state, shape_state),
        ],
        qkv, local, incoming, cotangent, halo, gain,
    )
    spec_sent = per_head((columns, 2, piece, hd), 3)
    shape_sent = whole((columns, 2, piece, width), bf16)
    early, local_k, local_v = call(
        grad_kernel,
        [spec_qkv, spec_total, per_head((1, total, hd), 2), spec_state, spec_taps, spec_rows],
        [
            (spec_sent, shape_sent),
            (spec_total, whole((total, width), f32)),
            (spec_total, whole((total, width), f32)),
        ],
        qkv, grad_norm, slope, incoming, conv_weight, attn_out,
    )
    early = lax.all_to_all(early, "head", 0, 0, tiled=True)
    future = scan(back, True)
    (late,) = call(
        last_kernel,
        [
            spec_qkv, pl.BlockSpec((1, total, hd), lambda h: (1, 0, h)),
            spec_total, spec_total, spec_state, spec_taps,
        ],
        [(spec_sent, shape_sent)],
        qkv, slope, local_k, local_v, future, conv_weight,
    )
    late = lax.all_to_all(late, "head", 0, 0, tiled=True)
    out, grad = pl.pallas_call(
        gather_kernel,
        out_shape=[
            whole((piece, columns * width), bf16),
            whole((3, piece, columns * width), bf16),
        ],
        compiler_params=pltpu.CompilerParams(vmem_limit_bytes=48 * 1024 * 1024),
    )(early, late)
    return out, grad.transpose(1, 0, 2)


def solution(mesh):
    return jax.shard_map(
        shards,
        mesh=mesh,
        in_specs=(P("seq", None, "head"), P(None, None, "head"), P("head"), P(), P("seq", "head")),
        out_specs=(P(("seq", "head"), None), P(("seq", "head"), None, None)),
        check_vma=False,
    )
```

```python
import functools

import jax
import jax.numpy as jnp
from jax import lax
from jax.experimental import pallas as pl
from jax.experimental.pallas import tpu as pltpu
from jax.sharding import PartitionSpec as P

HEAD_DIM = 128
TAPS = 4
CHUNK = 128
HALO = 16
EDGE = TAPS - 1
SHARE = 8
FAR = 1 << 30

f32 = jnp.float32
bf16 = jnp.bfloat16


def nt(a, b):
    return lax.dot_general(a, b, (((1,), (1,)), ((), ())), preferred_element_type=f32)


def nn(a, b):
    return lax.dot_general(a, b, (((1,), (0,)), ((), ())), preferred_element_type=f32)


def tn(a, b):
    return lax.dot_general(a, b, (((0,), (0,)), ((), ())), preferred_element_type=f32)


def doc_start(starts, first, pos):
    found = jnp.int32(-FAR)
    for d in range(starts.shape[0]):
        rel = starts[d] - first
        found = jnp.maximum(found, jnp.where(rel <= pos, rel, -FAR))
    return found


def doc_end(starts, first, pos):
    found = jnp.int32(FAR)
    for d in range(starts.shape[0]):
        rel = starts[d] - first
        found = jnp.minimum(found, jnp.where(rel > pos, rel, FAR))
    return found


def row_starts(starts, first, rows):
    found = jnp.full(rows.shape, -FAR, jnp.int32)
    for d in range(starts.shape[0]):
        rel = starts[d] - first
        found = jnp.maximum(found, jnp.where(rows >= rel, rel, -FAR))
    return found


def iota(shape, axis, base=0):
    return lax.broadcasted_iota(jnp.int32, shape, axis) + base


def conv_rows(ext, taps, m, age):
    conv = taps[m, 0:1] * ext
    for j in range(1, TAPS):
        conv = conv + jnp.where(age >= j, taps[m, j : j + 1] * pltpu.roll(ext, j, 0), 0.0)
    return conv


def logistic(x):
    return 1.0 / (1.0 + jnp.exp(-x))


def silu_slope(conv, sigma):
    return sigma * (1.0 + conv * (1.0 - sigma))


def conv_kernel(starts, raw, rim, cot, taps, qkv, message):
    rows = raw.shape[1]
    first = lax.axis_index("seq") * rows
    place = iota((HALO + rows, HEAD_DIM), 0, -HALO)
    age = place - row_starts(starts, first, place)
    made = []
    for m in range(3):
        ext = jnp.concatenate([rim[m], raw[m]], axis=0).astype(f32)
        conv = conv_rows(ext, taps, m, age)[HALO:]
        if m < 2:
            conv = conv * logistic(conv)
        made.append(conv.astype(bf16))
        qkv[m] = made[m]
    last = doc_start(starts, first, rows - 1)
    keep = iota((rows, HEAD_DIM), 0) >= last
    masked_k = jnp.where(keep, made[1], jnp.zeros((), bf16))
    summary = tn(masked_k, made[2])
    tops = [raw[m, :HALO].astype(f32) for m in range(3)] + [cot[...].astype(f32)]
    for n in range(message.shape[0]):
        row = tops[min(n // EDGE, 3)][n % EDGE : n % EDGE + 1]
        part = summary[n * SHARE : (n + 1) * SHARE]
        message[n] = jnp.concatenate([part, jnp.broadcast_to(row, part.shape)], axis=0).astype(bf16)


def slope_kernel(starts, raw, rim, taps, slope):
    rows = raw.shape[1]
    first = lax.axis_index("seq") * rows
    place = iota((HALO + rows, HEAD_DIM), 0, -HALO)
    age = place - row_starts(starts, first, place)
    for m in range(2):
        ext = jnp.concatenate([rim[m], raw[m]], axis=0).astype(f32)
        conv = conv_rows(ext, taps, m, age)[HALO:]
        slope[m] = silu_slope(conv, logistic(conv))


def local_kernel(starts, qkv, local):
    rows = qkv.shape[1]
    first = lax.axis_index("seq") * rows
    for low in range(0, rows, CHUNK):
        high = low + CHUNK
        start = doc_start(starts, first, low)
        scores = nt(qkv[0, low:high], qkv[1, :high])
        t, s = iota((CHUNK, high), 0, low), iota((CHUNK, high), 1)
        scores = jnp.where((s <= t) & (s >= start), scores, 0.0).astype(bf16)
        local[low:high] = nn(scores, qkv[2, :high])


def state_of(message):
    parts = message[...].astype(f32)[:, :SHARE]
    return parts.reshape(HEAD_DIM, HEAD_DIM).astype(bf16)


def normed(attn, gains, cots):
    msq = jnp.mean(attn * attn, axis=-1, keepdims=True)
    scale = lax.rsqrt(jnp.maximum(msq, 1.0))
    scaled = cots * gains
    inner = jnp.mean(scaled * attn, axis=-1, keepdims=True)
    factor = jnp.where(msq > 1.0, scale * scale * scale * inner, 0.0)
    return scale, (scale * scaled - attn * factor).astype(bf16)


def norm_kernel(starts, qkv, local, incoming, cot, gain, attn_out, grad_norm, back):
    rows = local.shape[0]
    first = lax.axis_index("seq") * rows
    prev = row_starts(starts, first, iota((rows, HEAD_DIM), 0)) < 0
    q = qkv[0]
    attn = local[...] + jnp.where(prev, nn(q, state_of(incoming)), 0.0)
    gains = gain[...]
    scale, grad = normed(attn, gains, cot[...].astype(f32))
    attn_out[...] = (attn * scale * gains).astype(bf16)
    grad_norm[...] = grad
    back[...] = tn(jnp.where(prev, q, jnp.zeros((), bf16)), grad)


def conv_back(grad, taps, m, age, rows):
    total = grad.shape[0]
    out = taps[m, 0:1] * grad[:rows]
    for j in range(1, TAPS):
        term = jnp.where(age >= j, taps[m, j : j + 1] * grad, 0.0)
        out = out + pltpu.roll(term, total - j, 0)[:rows]
    return out.astype(bf16)


def query_kernel(
    starts, qkv, grad_norm, slope, incoming, raw_end, taps, gain, attn_out,
    early, edge_qkv, edge_slope, edge_grad,
):
    rows = grad_norm.shape[0]
    total = rows + HALO
    first = lax.axis_index("seq") * rows
    place = iota((total, HEAD_DIM), 0)
    begin = row_starts(starts, first, place)
    age = place - begin
    state = state_of(incoming)
    k, v, g = qkv[1], qkv[2], grad_norm[...]

    line = iota((SHARE, HEAD_DIM), 0)

    def edge(a):
        block = jnp.zeros((SHARE, HEAD_DIM), f32)
        for n in range(EDGE):
            block = jnp.where(line == n, incoming[EDGE * a + n].astype(f32)[SHARE:], block)
        return jnp.concatenate([block, jnp.zeros((HALO - SHARE, HEAD_DIM), f32)], axis=0)

    edges, slopes = [], []
    for m in range(3):
        ext = jnp.concatenate([raw_end[m].astype(f32), edge(m)], axis=0)
        conv = conv_rows(ext, taps, m, age[rows - HALO :])[HALO:]
        if m < 2:
            sigma = logistic(conv)
            slopes.append(silu_slope(conv, sigma))
            conv = conv * sigma
        edges.append(conv.astype(bf16))
        edge_qkv[m] = edges[m]
    edge_slope[...] = slopes[1]
    q_e, k_e, v_e = edges
    start = doc_start(starts, first, rows)
    reach = iota((HALO, rows), 1) >= start
    causal = iota((HALO, HALO), 1) <= iota((HALO, HALO), 0)
    carry = begin[rows:] < 0

    def edge_sums(left, right, right_e, values, values_e, carried):
        scores = jnp.where(reach, nt(left, right), 0.0).astype(bf16)
        scores_e = jnp.where(causal, nt(left, right_e), 0.0).astype(bf16)
        return nn(scores, values) + nn(scores_e, values_e) + jnp.where(carry, carried, 0.0)

    attn_e = edge_sums(q_e, k, k_e, v, v_e, nn(q_e, state))
    _, g_e = normed(attn_e, gain[...], edge(3))
    edge_grad[...] = g_e
    grad_q_e = edge_sums(g_e, v, v_e, k, k_e, nt(g_e, state)) * slopes[0]

    parts = []
    for low in range(0, rows, CHUNK):
        high = low + CHUNK
        start = doc_start(starts, first, low)
        scores = nt(g[low:high], v[:high])
        t, s = iota((CHUNK, high), 0, low), iota((CHUNK, high), 1)
        scores = jnp.where((s <= t) & (s >= start), scores, 0.0).astype(bf16)
        parts.append(nn(scores, k[:high]))
    carried = jnp.where(begin[:rows] < 0, nt(g, state), 0.0)
    grad_q = (jnp.concatenate(parts, axis=0) + carried) * slope[0]
    out = conv_back(jnp.concatenate([grad_q, grad_q_e], axis=0), taps, 0, age, rows)
    shape = (early.shape[0], early.shape[2], HEAD_DIM)
    early[:, 0] = attn_out[...].reshape(shape)
    early[:, 1] = out.reshape(shape)


def key_kernel(starts, qkv, grad_norm, edge_qkv, edge_grad, local_k, local_v):
    rows = grad_norm.shape[0]
    first = lax.axis_index("seq") * rows
    q, k, v, g = qkv[0], qkv[1], qkv[2], grad_norm[...]
    for low in range(0, rows, CHUNK):
        high = low + CHUNK
        end = doc_end(starts, first, low)
        s, t = iota((CHUNK, rows - low), 0, low), iota((CHUNK, rows - low), 1, low)
        keep = (t >= s) & (t < end)
        scores = jnp.where(keep, nt(v[low:high], g[low:]), 0.0).astype(bf16)
        local_k[low:high] = nn(scores, q[low:])
        scores = jnp.where(keep, nt(k[low:high], q[low:]), 0.0).astype(bf16)
        local_v[low:high] = nn(scores, g[low:])
    q_e, k_e, v_e, g_e = edge_qkv[0], edge_qkv[1], edge_qkv[2], edge_grad[...]
    earlier = iota((HALO, HALO), 1) < iota((HALO, HALO), 0)
    scores = jnp.where(earlier, -nt(v_e, g_e), 0.0).astype(bf16)
    local_k[rows:] = nn(scores, q_e)
    scores = jnp.where(earlier, -nt(k_e, q_e), 0.0).astype(bf16)
    local_v[rows:] = nn(scores, g_e)


def last_kernel(
    starts, qkv, edge_qkv, slope, edge_slope, local_k, local_v, future, taps, early, late
):
    total = local_k.shape[0]
    rows = total - HALO
    first = lax.axis_index("seq") * rows
    place = iota((total, HEAD_DIM), 0)
    age = place - row_starts(starts, first, place)
    after = place >= doc_start(starts, first, rows)
    state = future[...].astype(bf16)
    slopes = jnp.concatenate([slope[0], edge_slope[...]], axis=0)
    k = jnp.concatenate([qkv[1], edge_qkv[1]], axis=0)
    v = jnp.concatenate([qkv[2], edge_qkv[2]], axis=0)
    grad_k = (local_k[...] + jnp.where(after, nt(v, state), 0.0)) * slopes
    grad_v = local_v[...] + jnp.where(after, nn(k, state), 0.0)
    shape = (late.shape[0], late.shape[2], HEAD_DIM)
    late[:, 0] = early[:, 0]
    late[:, 1] = early[:, 1]
    late[:, 2] = conv_back(grad_k, taps, 1, age, rows).reshape(shape)
    late[:, 3] = conv_back(grad_v, taps, 2, age, rows).reshape(shape)


def closed(starts, rows, i):
    found = jnp.bool_(False)
    for d in range(starts.shape[0]):
        found = found | ((starts[d] >= i * rows) & (starts[d] < (i + 1) * rows))
    return found


def forward_kernel(rows, starts, sums, out):
    count = sums.shape[0]
    state = jnp.zeros((SHARE, HEAD_DIM), f32)
    for i in range(count):
        here = sums[i].astype(f32)
        edge = sums[min(i + 1, count - 1)].astype(f32)[SHARE:]
        if i == count - 1:
            edge = jnp.zeros_like(edge)
        out[i] = jnp.concatenate([state, edge], axis=0).astype(bf16)
        state = here[:SHARE] + jnp.where(closed(starts, rows, i), 0.0, state)


def backward_kernel(rows, starts, sums, out):
    state = jnp.zeros(sums.shape[1:], f32)
    for i in range(sums.shape[0] - 1, -1, -1):
        out[i] = state
        state = sums[i] + jnp.where(closed(starts, rows, i), 0.0, state)


def gather_kernel(sent, out, grad):
    count, _, _, width = sent.shape
    for i in range(count):
        columns = slice(i * width, (i + 1) * width)
        out[:, columns] = sent[i, 0]
        for m in range(3):
            grad[m, :, columns] = sent[i, m + 1]


def shards(qkv_raw, conv_weight, norm_gain, doc_starts, cotangent):
    rows = qkv_raw.shape[0]
    width = qkv_raw.shape[2]
    heads = width // HEAD_DIM
    total = rows + HALO
    devices = lax.axis_size("seq")
    columns = lax.axis_size("head")
    piece = rows // columns
    share = devices // heads
    raw = qkv_raw.transpose(1, 0, 2)
    gain = norm_gain.reshape(1, width)
    in_hbm = functools.partial(pltpu.with_memory_space_constraint, memory_space=pltpu.HBM)
    doc_starts = pltpu.with_memory_space_constraint(doc_starts, pltpu.SMEM)
    hd = HEAD_DIM

    ahead = [(i, i + 1) for i in range(devices - 1)]
    rim = lax.ppermute(raw[:, rows - HALO :], "seq", ahead)

    smem = pl.BlockSpec(memory_space=pltpu.SMEM)
    params = pltpu.CompilerParams(vmem_limit_bytes=16 * 1024 * 1024)

    def block(shape, axis, **fixed):
        at = {int(name[1:]): index for name, index in fixed.items()}
        return pl.BlockSpec(
            shape, lambda h: tuple(h if a == axis else at.get(a, 0) for a in range(len(shape)))
        )

    def call(body, ins, outs, *args, grid=(heads,)):
        return pl.pallas_call(
            body,
            grid=grid,
            in_specs=[smem] + ins,
            out_specs=[spec for spec, _ in outs],
            out_shape=[shape for _, shape in outs],
            compiler_params=params,
        )(doc_starts, *args)

    def whole(dims, kind):
        return jax.ShapeDtypeStruct(dims, kind)

    spec_qkv = block((3, rows, hd), 2)
    spec_taps = block((3, TAPS, hd), 2)
    spec_rows = block((rows, hd), 1)
    spec_total = block((total, hd), 1)
    spec_state = block((hd, hd), 0)
    spec_message = block((share, 2 * SHARE, hd), 0)
    spec_gain = block((1, hd), 1)

    qkv, message = call(
        conv_kernel,
        [spec_qkv, block((3, HALO, hd), 2), block((HALO, hd), 1), spec_taps],
        [
            (spec_qkv, whole((3, rows, width), bf16)),
            (spec_message, whole((devices, 2 * SHARE, hd), bf16)),
        ],
        in_hbm(raw), rim, in_hbm(cotangent), in_hbm(conv_weight),
    )

    def swap(parts):
        return lax.all_to_all(parts, "seq", 0, 0, tiled=True)

    def scan(body, parts):
        flat = pl.BlockSpec(parts.shape, lambda: (0, 0, 0))
        (found,) = call(
            lambda *refs: body(rows, *refs), [flat], [(flat, whole(parts.shape, parts.dtype))],
            parts, grid=(),
        )
        return found

    (local,) = call(local_kernel, [spec_qkv], [(spec_rows, whole((rows, width), f32))], qkv)
    message, local = lax.optimization_barrier((swap(message), local))
    message = scan(forward_kernel, message)
    (slope,) = call(
        slope_kernel,
        [block((2, rows, hd), 2), block((2, HALO, hd), 2), spec_taps],
        [(block((2, rows, hd), 2), pltpu.HBM((2, rows, width), f32))],
        in_hbm(raw), rim, in_hbm(conv_weight),
    )
    incoming, slope = lax.optimization_barrier((swap(message), slope))
    attn_out, grad_norm, back = call(
        norm_kernel,
        [spec_qkv, spec_rows, spec_message, spec_rows, spec_gain],
        [
            (spec_rows, whole((rows, width), bf16)),
            (spec_rows, whole((rows, width), bf16)),
            (spec_state, whole((heads * hd, hd), f32)),
        ],
        qkv, local, incoming, cotangent, gain,
    )
    early, edge_qkv, edge_slope, edge_grad = call(
        query_kernel,
        [
            spec_qkv, spec_rows, block((1, rows, hd), 2), spec_message,
            block((3, HALO, hd), 2, a1=rows // HALO - 1), spec_taps, spec_gain, spec_rows,
        ],
        [
            (block((columns, 2, piece, hd), 3), whole((columns, 2, piece, width), bf16)),
            (block((3, HALO, hd), 2), whole((3, HALO, width), bf16)),
            (block((HALO, hd), 1), whole((HALO, width), f32)),
            (block((HALO, hd), 1), whole((HALO, width), bf16)),
        ],
        qkv, grad_norm, slope, incoming, in_hbm(raw), in_hbm(conv_weight), in_hbm(gain), attn_out,
    )
    back = swap(back.reshape(devices, SHARE, hd))
    back, early, edge_qkv, edge_slope, edge_grad = lax.optimization_barrier(
        (back, early, edge_qkv, edge_slope, edge_grad)
    )
    back = scan(backward_kernel, back)
    local_k, local_v = call(
        key_kernel,
        [spec_qkv, spec_rows, block((3, HALO, hd), 2), block((HALO, hd), 1)],
        [(spec_total, whole((total, width), f32))] * 2,
        qkv, grad_norm, edge_qkv, edge_grad,
    )
    future, local_k, local_v = lax.optimization_barrier((swap(back), local_k, local_v))
    (sent,) = call(
        last_kernel,
        [
            spec_qkv, block((3, HALO, hd), 2), block((1, rows, hd), 2, a0=1),
            block((HALO, hd), 1), spec_total, spec_total, spec_state, spec_taps,
            block((columns, 2, piece, hd), 3),
        ],
        [(block((columns, 4, piece, hd), 3), whole((columns, 4, piece, width), bf16))],
        qkv, edge_qkv, slope, edge_slope, local_k, local_v, future.reshape(heads * hd, hd),
        in_hbm(conv_weight), early,
    )
    sent = lax.all_to_all(sent, "head", 0, 0, tiled=True)
    out, grad = pl.pallas_call(
        gather_kernel,
        out_shape=[
            whole((piece, columns * width), bf16),
            whole((3, piece, columns * width), bf16),
        ],
        compiler_params=params,
    )(sent)
    return out, grad.transpose(1, 0, 2)


def solution(mesh):
    return jax.shard_map(
        shards,
        mesh=mesh,
        in_specs=(P("seq", None, "head"), P(None, None, "head"), P("head"), P(), P("seq", "head")),
        out_specs=(P(("seq", "head"), None), P(("seq", "head"), None, None)),
        check_vma=False,
    )
```

```python
import functools

import jax
import jax.numpy as jnp
from jax import lax
from jax.experimental import pallas as pl
from jax.experimental.pallas import tpu as pltpu
from jax.sharding import PartitionSpec as P

HEAD_DIM = 128
TAPS = 4
CHUNK = 128
HALO = 16
EDGE = TAPS - 1
SHARE = 8
FAR = 1 << 30

f32 = jnp.float32
bf16 = jnp.bfloat16


def nt(a, b):
    return lax.dot_general(a, b, (((1,), (1,)), ((), ())), preferred_element_type=f32)


def nn(a, b):
    return lax.dot_general(a, b, (((1,), (0,)), ((), ())), preferred_element_type=f32)


def tn(a, b):
    return lax.dot_general(a, b, (((0,), (0,)), ((), ())), preferred_element_type=f32)


def doc_start(starts, first, pos):
    found = jnp.int32(-FAR)
    for d in range(starts.shape[0]):
        rel = starts[d] - first
        found = jnp.maximum(found, jnp.where(rel <= pos, rel, -FAR))
    return found


def doc_end(starts, first, pos):
    found = jnp.int32(FAR)
    for d in range(starts.shape[0]):
        rel = starts[d] - first
        found = jnp.minimum(found, jnp.where(rel > pos, rel, FAR))
    return found


def row_starts(starts, first, rows):
    found = jnp.full(rows.shape, -FAR, jnp.int32)
    for d in range(starts.shape[0]):
        rel = starts[d] - first
        found = jnp.maximum(found, jnp.where(rows >= rel, rel, -FAR))
    return found


def iota(shape, axis, base=0):
    return lax.broadcasted_iota(jnp.int32, shape, axis) + base


def conv_rows(ext, taps, m, age):
    conv = taps[m, 0:1] * ext
    for j in range(1, TAPS):
        conv = conv + jnp.where(age >= j, taps[m, j : j + 1] * pltpu.roll(ext, j, 0), 0.0)
    return conv


def logistic(x):
    return 1.0 / (1.0 + jnp.exp(-x))


def silu_slope(conv, sigma):
    return sigma * (1.0 + conv * (1.0 - sigma))


def conv_docs(ext, taps, m, starts, first):
    rows = ext.shape[0] - HALO
    conv = taps[m, 0:1] * ext
    for j in range(1, TAPS):
        conv = conv + taps[m, j : j + 1] * pltpu.roll(ext, j, 0)
    parts = []
    for low in range(0, rows, CHUNK):
        top = ext[HALO + low - SHARE : HALO + low + SHARE]
        age = iota((2 * SHARE, HEAD_DIM), 0, low - SHARE) - doc_start(starts, first, low)
        parts.append(conv_rows(top, taps, m, age)[SHARE:])
        parts.append(conv[HALO + low + SHARE : HALO + low + CHUNK])
    return jnp.concatenate(parts, axis=0)


def head_columns(h):
    return slice(h * HEAD_DIM, (h + 1) * HEAD_DIM)


def conv_kernel(
    starts, raw_far, rim, cot_far, taps_far, gain_far,
    keys, values, message, raw_q, raw_end, taps, gain, raw, tops, sems,
):
    _, rows, width = raw.shape
    heads = range(width // HEAD_DIM)
    first = lax.axis_index("seq") * rows
    taps_load = pltpu.make_async_copy(taps_far, taps, sems.at[0])
    loads = [pltpu.make_async_copy(raw_far.at[m], raw.at[m - 1], sems.at[m]) for m in (1, 2)]
    others = [
        pltpu.make_async_copy(raw_far.at[:, pl.ds(0, HALO)], tops.at[pl.ds(0, 3)], sems.at[3]),
        pltpu.make_async_copy(cot_far.at[pl.ds(0, HALO)], tops.at[3], sems.at[4]),
        pltpu.make_async_copy(raw_far.at[:, pl.ds(rows - HALO, HALO)], raw_end, sems.at[5]),
        pltpu.make_async_copy(raw_far.at[0], raw_q, sems.at[6]),
        pltpu.make_async_copy(gain_far, gain, sems.at[7]),
    ]
    for load in [loads[0], taps_load, loads[1]] + others:
        load.start()
    taps_load.wait()
    keep = iota((rows, HEAD_DIM), 0) >= doc_start(starts, first, rows - 1)
    made = {}
    for m, out in ((1, keys), (2, values)):
        loads[m - 1].wait()
        for h in heads:
            at = head_columns(h)
            ext = jnp.concatenate([rim[m, :, at], raw[m - 1, :, at]], axis=0).astype(f32)
            conv = conv_docs(ext, taps.at[:, :, at], m, starts, first)
            if m == 1:
                conv = conv * logistic(conv)
            made[m, h] = conv.astype(bf16)
            out[:, at] = made[m, h]
    for load in others:
        load.wait()
    share = HEAD_DIM // SHARE
    for h in heads:
        at = head_columns(h)
        summary = tn(jnp.where(keep, made[1, h], jnp.zeros((), bf16)), made[2, h])
        for n in range(share):
            row = tops[min(n // EDGE, 3), :, at].astype(f32)[n % EDGE : n % EDGE + 1]
            part = summary[n * SHARE : (n + 1) * SHARE]
            both = jnp.concatenate([part, jnp.broadcast_to(row, part.shape)], axis=0)
            message[h * share + n] = both.astype(bf16)


def slope_kernel(starts, raw_far, rim, taps, slope_q, slope_k, raw, sems):
    _, rows, width = raw.shape
    first = lax.axis_index("seq") * rows
    loads = [pltpu.make_async_copy(raw_far.at[m], raw.at[m], sems.at[m]) for m in range(2)]
    for load in loads:
        load.start()
    for m, out in ((0, slope_q), (1, slope_k)):
        loads[m].wait()
        for h in range(width // HEAD_DIM):
            at = head_columns(h)
            ext = jnp.concatenate([rim[m, :, at], raw[m, :, at]], axis=0).astype(f32)
            conv = conv_docs(ext, taps.at[:, :, at], m, starts, first)
            out[:, at] = silu_slope(conv, logistic(conv))


def local_kernel(starts, raw_q, rim, taps, keys, values, queries, local):
    rows, width = local.shape
    first = lax.axis_index("seq") * rows
    for h in range(width // HEAD_DIM):
        at = head_columns(h)
        ext = jnp.concatenate([rim[0, :, at], raw_q[:, at]], axis=0).astype(f32)
        conv = conv_docs(ext, taps.at[:, :, at], 0, starts, first)
        q = (conv * logistic(conv)).astype(bf16)
        queries[:, at] = q
        for low in range(0, rows, CHUNK):
            high = low + CHUNK
            start = doc_start(starts, first, low)
            scores = nt(q[low:high], keys[:high, at])
            t, s = iota((CHUNK, high), 0, low), iota((CHUNK, high), 1)
            scores = jnp.where((s <= t) & (s >= start), scores, 0.0).astype(bf16)
            local[low:high, at] = nn(scores, values[:high, at])


def state_of(message):
    return message.astype(f32)[:, :SHARE].reshape(HEAD_DIM, HEAD_DIM).astype(bf16)


def normed(attn, gains, cots):
    msq = jnp.mean(attn * attn, axis=-1, keepdims=True)
    scale = lax.rsqrt(jnp.maximum(msq, 1.0))
    scaled = cots * gains
    inner = jnp.mean(scaled * attn, axis=-1, keepdims=True)
    factor = jnp.where(msq > 1.0, scale * scale * scale * inner, 0.0)
    return scale, (scale * scaled - attn * factor).astype(bf16)


def norm_kernel(
    starts, queries, local, incoming, cot, gain, attn_out, grad_norm, back
):
    rows, width = local.shape
    heads = range(width // HEAD_DIM)
    share = HEAD_DIM // SHARE
    first = lax.axis_index("seq") * rows
    prev = row_starts(starts, first, iota((rows, HEAD_DIM), 0)) < 0
    attns = []
    for h in heads:
        at = head_columns(h)
        carried = nn(queries[:, at], state_of(incoming[h * share : (h + 1) * share]))
        attns.append(local[:, at] + jnp.where(prev, carried, 0.0))
    for h in heads:
        at = head_columns(h)
        scale, grad = normed(attns[h], gain[:, at], cot[:, at].astype(f32))
        out = (attns[h] * scale * gain[:, at]).astype(bf16)
        attn_out[:, :, at] = out.reshape(attn_out.shape[:2] + (HEAD_DIM,))
        grad_norm[:, at] = grad
        masked_q = jnp.where(prev, queries[:, at], jnp.zeros((), bf16))
        back[h * HEAD_DIM : (h + 1) * HEAD_DIM] = tn(masked_q, grad).astype(bf16)


def conv_back(grad, taps, m, starts, first, rows):
    total = grad.shape[0]
    out = taps[m, 0:1] * grad[:rows]
    for j in range(1, TAPS):
        out = out + pltpu.roll(taps[m, j : j + 1] * grad, total - j, 0)[:rows]
    parts = []
    for high in range(CHUNK, rows + 1, CHUNK):
        near = grad[high - SHARE : high + SHARE]
        age = iota((2 * SHARE, HEAD_DIM), 0, high - SHARE)
        age = age - row_starts(starts, first, age)
        end = taps[m, 0:1] * near[:SHARE]
        for j in range(1, TAPS):
            term = jnp.where(age >= j, taps[m, j : j + 1] * near, 0.0)
            end = end + pltpu.roll(term, 2 * SHARE - j, 0)[:SHARE]
        parts.append(out[high - CHUNK : high - SHARE])
        parts.append(end)
    return jnp.concatenate(parts, axis=0).astype(bf16)


def edge_rows(incoming, a):
    line = iota((SHARE, HEAD_DIM), 0)
    block = jnp.zeros((SHARE, HEAD_DIM), f32)
    for n in range(EDGE):
        block = jnp.where(line == n, incoming[EDGE * a + n].astype(f32)[SHARE:], block)
    return jnp.concatenate([block, jnp.zeros((HALO - SHARE, HEAD_DIM), f32)], axis=0)


def query_kernel(
    starts, keys, values, grad_norm, slope, incoming, raw_end, taps, gain, attn_out,
    early, edge_qkv, edge_slope, edge_grad, out_rows, sems,
):
    rows, width = grad_norm.shape
    heads = range(width // HEAD_DIM)
    share = HEAD_DIM // SHARE
    first = lax.axis_index("seq") * rows
    stores = [pltpu.make_async_copy(attn_out, early.at[:, 0], sems.at[0])]
    stores[0].start()
    carry = row_starts(starts, first, iota((rows, HEAD_DIM), 0)) < 0
    start = doc_start(starts, first, rows)
    edge_age = iota((2 * HALO, HEAD_DIM), 0, rows - HALO)
    edge_age = edge_age - row_starts(starts, first, edge_age)
    reach = iota((HALO, rows), 1) >= start
    causal = iota((HALO, HALO), 1) <= iota((HALO, HALO), 0)
    for h in heads:
        at = head_columns(h)
        heard = incoming.at[pl.ds(h * share, share)]
        state = state_of(heard[...])
        k, v, g = keys[:, at], values[:, at], grad_norm[:, at]
        edges, slopes = [], []
        for m in range(3):
            ext = jnp.concatenate([raw_end[m, :, at].astype(f32), edge_rows(heard, m)], axis=0)
            conv = conv_rows(ext, taps.at[:, :, at], m, edge_age)[HALO:]
            if m < 2:
                sigma = logistic(conv)
                slopes.append(silu_slope(conv, sigma))
                conv = conv * sigma
            edges.append(conv.astype(bf16))
            edge_qkv[m, :, at] = edges[m]
        edge_slope[:, at] = slopes[1]
        q_e, k_e, v_e = edges

        def edge_sums(left, right, right_e, values, values_e, carried):
            scores = jnp.where(reach, nt(left, right), 0.0).astype(bf16)
            scores_e = jnp.where(causal, nt(left, right_e), 0.0).astype(bf16)
            added = jnp.where(start < 0, carried, 0.0)
            return nn(scores, values) + nn(scores_e, values_e) + added

        attn_e = edge_sums(q_e, k, k_e, v, v_e, nn(q_e, state))
        _, g_e = normed(attn_e, gain[:, at], edge_rows(heard, 3))
        edge_grad[:, at] = g_e
        grad_q_e = edge_sums(g_e, v, v_e, k, k_e, nt(g_e, state)) * slopes[0]

        parts = []
        for low in range(0, rows, CHUNK):
            high = low + CHUNK
            begin = doc_start(starts, first, low)
            scores = nt(g[low:high], v[:high])
            t, s = iota((CHUNK, high), 0, low), iota((CHUNK, high), 1)
            scores = jnp.where((s <= t) & (s >= begin), scores, 0.0).astype(bf16)
            parts.append(nn(scores, k[:high]))
        carried = jnp.where(carry, nt(g, state), 0.0)
        grad_q = (jnp.concatenate(parts, axis=0) + carried) * slope[:, at]
        both = jnp.concatenate([grad_q, grad_q_e], axis=0)
        out = conv_back(both, taps.at[:, :, at], 0, starts, first, rows)
        out_rows[:, :, at] = out.reshape(out_rows.shape[:2] + (HEAD_DIM,))
        lanes = pl.ds(h * HEAD_DIM, HEAD_DIM)
        part = out_rows.at[:, :, lanes]
        stores.append(pltpu.make_async_copy(part, early.at[:, 1, :, lanes], sems.at[h + 1]))
        stores[-1].start()
    for store in stores:
        store.wait()


def key_kernel(starts, queries, keys, values, grad_norm, edge_qkv, edge_grad, local_k, local_v):
    rows, width = grad_norm.shape
    first = lax.axis_index("seq") * rows
    for h in range(width // HEAD_DIM):
        at = head_columns(h)
        q, k, v, g = queries[:, at], keys[:, at], values[:, at], grad_norm[:, at]
        for low in range(0, rows, CHUNK):
            high = low + CHUNK
            end = doc_end(starts, first, low)
            s, t = iota((CHUNK, rows - low), 0, low), iota((CHUNK, rows - low), 1, low)
            keep = (t >= s) & (t < end)
            scores = jnp.where(keep, nt(v[low:high], g[low:]), 0.0).astype(bf16)
            local_k[low:high, at] = nn(scores, q[low:])
            scores = jnp.where(keep, nt(k[low:high], q[low:]), 0.0).astype(bf16)
            local_v[low:high, at] = nn(scores, g[low:])
        q_e, k_e, v_e = edge_qkv[0, :, at], edge_qkv[1, :, at], edge_qkv[2, :, at]
        g_e = edge_grad[:, at]
        earlier = iota((HALO, HALO), 1) < iota((HALO, HALO), 0)
        scores = jnp.where(earlier, -nt(v_e, g_e), 0.0).astype(bf16)
        local_k[rows:, at] = nn(scores, q_e)
        scores = jnp.where(earlier, -nt(k_e, q_e), 0.0).astype(bf16)
        local_v[rows:, at] = nn(scores, g_e)


def last_kernel(
    starts, keys, values, edge_qkv, slope, edge_slope, local_k, local_v, future, taps, early,
    sent, sem,
):
    total, width = local_k.shape
    rows = total - HALO
    first = lax.axis_index("seq") * rows
    copy = pltpu.make_async_copy(early, sent.at[:, pl.ds(0, 2)], sem)
    copy.start()
    after = iota((total, HEAD_DIM), 0) >= doc_start(starts, first, rows)
    shape = (sent.shape[0], sent.shape[2], HEAD_DIM)
    for h in range(width // HEAD_DIM):
        at = head_columns(h)
        state = future[h * HEAD_DIM : (h + 1) * HEAD_DIM]
        k = jnp.concatenate([keys[:, at], edge_qkv[1, :, at]], axis=0)
        v = jnp.concatenate([values[:, at], edge_qkv[2, :, at]], axis=0)
        slopes = jnp.concatenate([slope[:, at], edge_slope[:, at]], axis=0)
        grad_k = (local_k[:, at] + jnp.where(after, nt(v, state), 0.0)) * slopes
        grad_v = local_v[:, at] + jnp.where(after, nn(k, state), 0.0)
        for m, grad in ((1, grad_k), (2, grad_v)):
            out = conv_back(grad, taps.at[:, :, at], m, starts, first, rows)
            sent[:, m + 1, :, at] = out.reshape(shape)
    copy.wait()


def closed(starts, rows, i):
    found = jnp.bool_(False)
    for d in range(starts.shape[0]):
        found = found | ((starts[d] >= i * rows) & (starts[d] < (i + 1) * rows))
    return found


def forward_kernel(rows, starts, sums, out):
    count = sums.shape[0]
    state = jnp.zeros((SHARE, HEAD_DIM), f32)
    for i in range(count):
        here = sums[i].astype(f32)
        edge = sums[min(i + 1, count - 1)].astype(f32)[SHARE:]
        if i == count - 1:
            edge = jnp.zeros_like(edge)
        out[i] = jnp.concatenate([state, edge], axis=0).astype(bf16)
        state = here[:SHARE] + jnp.where(closed(starts, rows, i), 0.0, state)


def backward_kernel(rows, starts, sums, out):
    count = 2 * sums.shape[0]
    state = jnp.zeros((SHARE, HEAD_DIM), f32)
    for i in range(count - 1, 0, -2):
        pair = sums[i // 2].astype(f32)
        upper = state
        state = pair[SHARE:] + jnp.where(closed(starts, rows, i), 0.0, state)
        out[i // 2] = jnp.concatenate([state, upper], axis=0).astype(bf16)
        state = pair[:SHARE] + jnp.where(closed(starts, rows, i - 1), 0.0, state)


def gather_kernel(sent, out, grad):
    count, _, _, width = sent.shape
    for i in range(count):
        columns = slice(i * width, (i + 1) * width)
        out[:, columns] = sent[i, 0]
        for m in range(3):
            grad[m, :, columns] = sent[i, m + 1]


def shards(qkv_raw, conv_weight, norm_gain, doc_starts, cotangent):
    rows = qkv_raw.shape[0]
    width = qkv_raw.shape[2]
    heads = width // HEAD_DIM
    total = rows + HALO
    devices = lax.axis_size("seq")
    columns = lax.axis_size("head")
    piece = rows // columns
    share = devices // heads
    raw = qkv_raw.transpose(1, 0, 2)
    in_hbm = functools.partial(pltpu.with_memory_space_constraint, memory_space=pltpu.HBM)
    doc_starts = pltpu.with_memory_space_constraint(doc_starts, pltpu.SMEM)
    hd = HEAD_DIM

    ahead = [(i, i + 1) for i in range(devices - 1)]
    rim = lax.ppermute(raw[:, rows - HALO :], "seq", ahead)

    smem = pl.BlockSpec(memory_space=pltpu.SMEM)
    params = pltpu.CompilerParams(vmem_limit_bytes=16 * 1024 * 1024)

    vmem = pl.BlockSpec(memory_space=pltpu.VMEM)
    hbm = pl.BlockSpec(memory_space=pltpu.HBM)
    dma = pltpu.SemaphoreType.DMA

    def flat_call(body, ins, outs, scratch, *args, alias={}):
        return pl.pallas_call(
            body,
            in_specs=[smem] + ins,
            out_specs=[hbm if out.memory_space == pltpu.HBM else vmem for out in outs],
            out_shape=outs,
            scratch_shapes=scratch,
            input_output_aliases=alias,
            compiler_params=params,
        )(doc_starts, *[in_hbm(a) if spec is hbm else a for a, spec in zip(args, ins)])

    wide = pltpu.VMEM((rows, width), bf16)
    keys, values, message, raw_q, raw_end, taps, gain = flat_call(
        conv_kernel,
        [hbm, vmem, hbm, hbm, hbm],
        [
            wide, wide, pltpu.VMEM((devices, 2 * SHARE, hd), bf16), wide,
            pltpu.VMEM((3, HALO, width), bf16), pltpu.VMEM(conv_weight.shape, f32),
            pltpu.VMEM((1, width), f32),
        ],
        [pltpu.VMEM((2, rows, width), bf16), pltpu.VMEM((4, HALO, width), bf16), dma((8,))],
        raw, rim, cotangent, conv_weight, norm_gain.reshape(1, width),
    )

    def swap(parts):
        return lax.all_to_all(parts, "seq", 0, 0, tiled=True)

    def scan(body, parts):
        (found,) = flat_call(
            functools.partial(body, rows), [vmem], [pltpu.VMEM(parts.shape, bf16)], [], parts
        )
        return found

    queries, local = flat_call(
        local_kernel, [vmem] * 5, [wide, pltpu.VMEM((rows, width), f32)], [],
        raw_q, rim, taps, keys, values,
    )
    message, queries, local = lax.optimization_barrier((swap(message), queries, local))
    message = scan(forward_kernel, message)
    slope_q, slope_k = flat_call(
        slope_kernel, [hbm, vmem, vmem], [pltpu.VMEM((rows, width), f32)] * 2,
        [pltpu.VMEM((2, rows, width), bf16), dma((2,))],
        raw, rim, taps,
    )
    incoming, slope_q, slope_k = lax.optimization_barrier((swap(message), slope_q, slope_k))
    attn_out, grad_norm, back = flat_call(
        norm_kernel,
        [vmem] * 5,
        [
            pltpu.VMEM((columns, piece, width), bf16), pltpu.VMEM((rows, width), bf16),
            pltpu.VMEM((heads * hd, hd), bf16),
        ],
        [],
        queries, local, incoming, cotangent, gain,
    )
    early, edge_qkv, edge_slope, edge_grad = flat_call(
        query_kernel,
        [vmem] * 9,
        [
            pltpu.HBM((columns, 2, piece, width), bf16), pltpu.VMEM((3, HALO, width), bf16),
            pltpu.VMEM((HALO, width), f32), pltpu.VMEM((HALO, width), bf16),
        ],
        [pltpu.VMEM((columns, piece, width), bf16), dma((heads + 1,))],
        keys, values, grad_norm, slope_q, incoming, raw_end, taps, gain, attn_out,
    )
    back = swap(back.reshape(devices, SHARE, hd))
    back, early, edge_qkv, edge_slope, edge_grad = lax.optimization_barrier(
        (back, early, edge_qkv, edge_slope, edge_grad)
    )
    back = scan(backward_kernel, back.reshape(devices // 2, 2 * SHARE, hd))
    local_k, local_v = flat_call(
        key_kernel, [vmem] * 6, [pltpu.VMEM((total, width), f32)] * 2, [],
        queries, keys, values, grad_norm, edge_qkv, edge_grad,
    )
    future, local_k, local_v = lax.optimization_barrier((swap(back.reshape(devices, SHARE, hd)), local_k, local_v))
    (sent,) = flat_call(
        last_kernel, [vmem] * 9 + [hbm], [pltpu.VMEM((columns, 4, piece, width), bf16)], [dma(())],
        keys, values, edge_qkv, slope_k, edge_slope, local_k, local_v,
        future.reshape(heads * hd, hd), taps, early,
    )
    sent = lax.all_to_all(sent, "head", 0, 0, tiled=True)
    out, grad = pl.pallas_call(
        gather_kernel,
        out_shape=[
            jax.ShapeDtypeStruct((piece, columns * width), bf16),
            jax.ShapeDtypeStruct((3, piece, columns * width), bf16),
        ],
        compiler_params=params,
    )(sent)
    return out, grad.transpose(1, 0, 2)


def solution(mesh):
    return jax.shard_map(
        shards,
        mesh=mesh,
        in_specs=(P("seq", None, "head"), P(None, None, "head"), P("head"), P(), P("seq", "head")),
        out_specs=(P(("seq", "head"), None), P(("seq", "head"), None, None)),
        check_vma=False,
    )
```

```python
import functools

import jax
import jax.numpy as jnp
from jax import lax
from jax.experimental import pallas as pl
from jax.experimental.pallas import tpu as pltpu
from jax.sharding import PartitionSpec as P

HEAD_DIM = 128
TAPS = 4
CHUNK = 128
HALO = 16
EDGE = TAPS - 1
SHARE = 8
FAR = 1 << 30

f32 = jnp.float32
bf16 = jnp.bfloat16


def nt(a, b):
    return lax.dot_general(a, b, (((1,), (1,)), ((), ())), preferred_element_type=f32)


def nn(a, b):
    return lax.dot_general(a, b, (((1,), (0,)), ((), ())), preferred_element_type=f32)


def tn(a, b):
    return lax.dot_general(a, b, (((0,), (0,)), ((), ())), preferred_element_type=f32)


def doc_start(starts, first, pos):
    found = jnp.int32(-FAR)
    for d in range(starts.shape[0]):
        rel = starts[d] - first
        found = jnp.maximum(found, jnp.where(rel <= pos, rel, -FAR))
    return found


def doc_end(starts, first, pos):
    found = jnp.int32(FAR)
    for d in range(starts.shape[0]):
        rel = starts[d] - first
        found = jnp.minimum(found, jnp.where(rel > pos, rel, FAR))
    return found


def row_starts(starts, first, rows):
    found = jnp.full(rows.shape, -FAR, jnp.int32)
    for d in range(starts.shape[0]):
        rel = starts[d] - first
        found = jnp.maximum(found, jnp.where(rows >= rel, rel, -FAR))
    return found


def iota(shape, axis, base=0):
    return lax.broadcasted_iota(jnp.int32, shape, axis) + base


def conv_rows(ext, taps, m, age):
    conv = taps[m, 0:1] * ext
    for j in range(1, TAPS):
        conv = conv + jnp.where(age >= j, taps[m, j : j + 1] * pltpu.roll(ext, j, 0), 0.0)
    return conv


def logistic(x):
    return 1.0 / (1.0 + jnp.exp(-x))


def silu_slope(conv, sigma):
    return sigma * (1.0 + conv * (1.0 - sigma))


def conv_docs(ext, taps, m, starts, first):
    rows = ext.shape[0] - HALO
    conv = taps[m, 0:1] * ext
    for j in range(1, TAPS):
        conv = conv + taps[m, j : j + 1] * pltpu.roll(ext, j, 0)
    parts = []
    for low in range(0, rows, CHUNK):
        top = ext[HALO + low - SHARE : HALO + low + SHARE]
        age = iota((2 * SHARE, HEAD_DIM), 0, low - SHARE) - doc_start(starts, first, low)
        parts.append(conv_rows(top, taps, m, age)[SHARE:])
        parts.append(conv[HALO + low + SHARE : HALO + low + CHUNK])
    return jnp.concatenate(parts, axis=0)


def head_columns(h):
    return slice(h * HEAD_DIM, (h + 1) * HEAD_DIM)


def fetch_kernel(starts, raw_far, cot_far, taps_far, gain_far, raw, raw_end, tops, taps, gain, sems):
    rows = raw.shape[1]
    loads = [
        (raw_far, raw),
        (raw_far.at[:, pl.ds(rows - HALO, HALO)], raw_end),
        (raw_far.at[:, pl.ds(0, HALO)], tops.at[pl.ds(0, 3)]),
        (cot_far.at[pl.ds(0, HALO)], tops.at[3]),
        (taps_far, taps),
        (gain_far, gain),
    ]
    loads = [pltpu.make_async_copy(*ends, sems.at[n]) for n, ends in enumerate(loads)]
    for load in loads:
        load.start()
    for load in loads:
        load.wait()


def conv_kernel(starts, raw, rim, tops, taps, keys, values, message):
    _, rows, width = raw.shape
    heads = range(width // HEAD_DIM)
    first = lax.axis_index("seq") * rows
    keep = iota((rows, HEAD_DIM), 0) >= doc_start(starts, first, rows - 1)
    made = {}
    for m, out in ((1, keys), (2, values)):
        for h in heads:
            at = head_columns(h)
            ext = jnp.concatenate([rim[m, :, at], raw[m, :, at]], axis=0).astype(f32)
            conv = conv_docs(ext, taps.at[:, :, at], m, starts, first)
            if m == 1:
                conv = conv * logistic(conv)
            made[m, h] = conv.astype(bf16)
            out[:, at] = made[m, h]
    share = HEAD_DIM // SHARE
    for h in heads:
        at = head_columns(h)
        summary = tn(jnp.where(keep, made[1, h], jnp.zeros((), bf16)), made[2, h])
        for n in range(share):
            row = tops[min(n // EDGE, 3), :, at].astype(f32)[n % EDGE : n % EDGE + 1]
            part = summary[n * SHARE : (n + 1) * SHARE]
            both = jnp.concatenate([part, jnp.broadcast_to(row, part.shape)], axis=0)
            message[h * share + n] = both.astype(bf16)


def slope_kernel(starts, raw, rim, taps, slope_q, slope_k):
    _, rows, width = raw.shape
    first = lax.axis_index("seq") * rows
    for m, out in ((0, slope_q), (1, slope_k)):
        for h in range(width // HEAD_DIM):
            at = head_columns(h)
            ext = jnp.concatenate([rim[m, :, at], raw[m, :, at]], axis=0).astype(f32)
            conv = conv_docs(ext, taps.at[:, :, at], m, starts, first)
            out[:, at] = silu_slope(conv, logistic(conv))


def local_kernel(starts, raw, rim, taps, keys, values, queries, local):
    rows, width = local.shape
    first = lax.axis_index("seq") * rows
    for h in range(width // HEAD_DIM):
        at = head_columns(h)
        ext = jnp.concatenate([rim[0, :, at], raw[0, :, at]], axis=0).astype(f32)
        conv = conv_docs(ext, taps.at[:, :, at], 0, starts, first)
        q = (conv * logistic(conv)).astype(bf16)
        queries[:, at] = q
        for low in range(0, rows, CHUNK):
            high = low + CHUNK
            start = doc_start(starts, first, low)
            scores = nt(q[low:high], keys[:high, at])
            t, s = iota((CHUNK, high), 0, low), iota((CHUNK, high), 1)
            scores = jnp.where((s <= t) & (s >= start), scores, 0.0).astype(bf16)
            local[low:high, at] = nn(scores, values[:high, at])


def state_of(message):
    return message.astype(f32)[:, :SHARE].reshape(HEAD_DIM, HEAD_DIM).astype(bf16)


def normed(attn, gains, cots):
    msq = jnp.mean(attn * attn, axis=-1, keepdims=True)
    scale = lax.rsqrt(jnp.maximum(msq, 1.0))
    scaled = cots * gains
    inner = jnp.mean(scaled * attn, axis=-1, keepdims=True)
    factor = jnp.where(msq > 1.0, scale * scale * scale * inner, 0.0)
    return scale, (scale * scaled - attn * factor).astype(bf16)


def norm_kernel(
    starts, queries, local, incoming, cot, gain, attn_out, grad_norm, back
):
    rows, width = local.shape
    heads = range(width // HEAD_DIM)
    share = HEAD_DIM // SHARE
    first = lax.axis_index("seq") * rows
    prev = row_starts(starts, first, iota((rows, HEAD_DIM), 0)) < 0
    attns = []
    for h in heads:
        at = head_columns(h)
        carried = nn(queries[:, at], state_of(incoming[h * share : (h + 1) * share]))
        attns.append(local[:, at] + jnp.where(prev, carried, 0.0))
    for h in heads:
        at = head_columns(h)
        scale, grad = normed(attns[h], gain[:, at], cot[:, at].astype(f32))
        out = (attns[h] * scale * gain[:, at]).astype(bf16)
        attn_out[:, :, at] = out.reshape(attn_out.shape[:2] + (HEAD_DIM,))
        grad_norm[:, at] = grad
        masked_q = jnp.where(prev, queries[:, at], jnp.zeros((), bf16))
        back[h * HEAD_DIM : (h + 1) * HEAD_DIM] = tn(masked_q, grad).astype(bf16)


def conv_back(grad, taps, m, starts, first, rows):
    total = grad.shape[0]
    out = taps[m, 0:1] * grad[:rows]
    for j in range(1, TAPS):
        out = out + pltpu.roll(taps[m, j : j + 1] * grad, total - j, 0)[:rows]
    parts = []
    for high in range(CHUNK, rows + 1, CHUNK):
        near = grad[high - SHARE : high + SHARE]
        age = iota((2 * SHARE, HEAD_DIM), 0, high - SHARE)
        age = age - row_starts(starts, first, age)
        end = taps[m, 0:1] * near[:SHARE]
        for j in range(1, TAPS):
            term = jnp.where(age >= j, taps[m, j : j + 1] * near, 0.0)
            end = end + pltpu.roll(term, 2 * SHARE - j, 0)[:SHARE]
        parts.append(out[high - CHUNK : high - SHARE])
        parts.append(end)
    return jnp.concatenate(parts, axis=0).astype(bf16)


def edge_rows(incoming, a):
    line = iota((SHARE, HEAD_DIM), 0)
    block = jnp.zeros((SHARE, HEAD_DIM), f32)
    for n in range(EDGE):
        block = jnp.where(line == n, incoming[EDGE * a + n].astype(f32)[SHARE:], block)
    return jnp.concatenate([block, jnp.zeros((HALO - SHARE, HEAD_DIM), f32)], axis=0)


def query_kernel(
    starts, keys, values, grad_norm, slope, incoming, raw_end, taps, gain, attn_out,
    early, edge_qkv, edge_slope, edge_grad, sem,
):
    rows, width = grad_norm.shape
    heads = range(width // HEAD_DIM)
    share = HEAD_DIM // SHARE
    first = lax.axis_index("seq") * rows
    copy = pltpu.make_async_copy(attn_out, early.at[:, 0], sem)
    copy.start()
    carry = row_starts(starts, first, iota((rows, HEAD_DIM), 0)) < 0
    start = doc_start(starts, first, rows)
    edge_age = iota((2 * HALO, HEAD_DIM), 0, rows - HALO)
    edge_age = edge_age - row_starts(starts, first, edge_age)
    reach = iota((HALO, rows), 1) >= start
    causal = iota((HALO, HALO), 1) <= iota((HALO, HALO), 0)
    for h in heads:
        at = head_columns(h)
        heard = incoming.at[pl.ds(h * share, share)]
        state = state_of(heard[...])
        k, v, g = keys[:, at], values[:, at], grad_norm[:, at]
        edges, slopes = [], []
        for m in range(3):
            ext = jnp.concatenate([raw_end[m, :, at].astype(f32), edge_rows(heard, m)], axis=0)
            conv = conv_rows(ext, taps.at[:, :, at], m, edge_age)[HALO:]
            if m < 2:
                sigma = logistic(conv)
                slopes.append(silu_slope(conv, sigma))
                conv = conv * sigma
            edges.append(conv.astype(bf16))
            edge_qkv[m, :, at] = edges[m]
        edge_slope[:, at] = slopes[1]
        q_e, k_e, v_e = edges

        def edge_sums(left, right, right_e, values, values_e, carried):
            scores = jnp.where(reach, nt(left, right), 0.0).astype(bf16)
            scores_e = jnp.where(causal, nt(left, right_e), 0.0).astype(bf16)
            added = jnp.where(start < 0, carried, 0.0)
            return nn(scores, values) + nn(scores_e, values_e) + added

        attn_e = edge_sums(q_e, k, k_e, v, v_e, nn(q_e, state))
        _, g_e = normed(attn_e, gain[:, at], edge_rows(heard, 3))
        edge_grad[:, at] = g_e
        grad_q_e = edge_sums(g_e, v, v_e, k, k_e, nt(g_e, state)) * slopes[0]

        parts = []
        for low in range(0, rows, CHUNK):
            high = low + CHUNK
            begin = doc_start(starts, first, low)
            scores = nt(g[low:high], v[:high])
            t, s = iota((CHUNK, high), 0, low), iota((CHUNK, high), 1)
            scores = jnp.where((s <= t) & (s >= begin), scores, 0.0).astype(bf16)
            parts.append(nn(scores, k[:high]))
        carried = jnp.where(carry, nt(g, state), 0.0)
        grad_q = (jnp.concatenate(parts, axis=0) + carried) * slope[:, at]
        both = jnp.concatenate([grad_q, grad_q_e], axis=0)
        out = conv_back(both, taps.at[:, :, at], 0, starts, first, rows)
        early[:, 1, :, at] = out.reshape((early.shape[0], early.shape[2], HEAD_DIM))
    copy.wait()


def key_kernel(starts, queries, keys, values, grad_norm, edge_qkv, edge_grad, local_k, local_v):
    rows, width = grad_norm.shape
    first = lax.axis_index("seq") * rows
    for h in range(width // HEAD_DIM):
        at = head_columns(h)
        q, k, v, g = queries[:, at], keys[:, at], values[:, at], grad_norm[:, at]
        for low in range(0, rows, CHUNK):
            high = low + CHUNK
            end = doc_end(starts, first, low)
            s, t = iota((CHUNK, rows - low), 0, low), iota((CHUNK, rows - low), 1, low)
            keep = (t >= s) & (t < end)
            scores = jnp.where(keep, nt(v[low:high], g[low:]), 0.0).astype(bf16)
            local_k[low:high, at] = nn(scores, q[low:]).astype(bf16)
            scores = jnp.where(keep, nt(k[low:high], q[low:]), 0.0).astype(bf16)
            local_v[low:high, at] = nn(scores, g[low:]).astype(bf16)
        q_e, k_e, v_e = edge_qkv[0, :, at], edge_qkv[1, :, at], edge_qkv[2, :, at]
        g_e = edge_grad[:, at]
        earlier = iota((HALO, HALO), 1) < iota((HALO, HALO), 0)
        scores = jnp.where(earlier, -nt(v_e, g_e), 0.0).astype(bf16)
        local_k[rows:, at] = nn(scores, q_e).astype(bf16)
        scores = jnp.where(earlier, -nt(k_e, q_e), 0.0).astype(bf16)
        local_v[rows:, at] = nn(scores, g_e).astype(bf16)


def last_kernel(
    starts, keys, values, edge_qkv, slope, edge_slope, local_k, local_v, future, taps, early,
    sent, sem,
):
    total, width = local_k.shape
    rows = total - HALO
    first = lax.axis_index("seq") * rows
    copy = pltpu.make_async_copy(early, sent.at[:, pl.ds(0, 2)], sem)
    copy.start()
    after = iota((total, HEAD_DIM), 0) >= doc_start(starts, first, rows)
    shape = (sent.shape[0], sent.shape[2], HEAD_DIM)
    for m in (2, 1):
        for h in range(width // HEAD_DIM):
            at = head_columns(h)
            state = future[h * HEAD_DIM : (h + 1) * HEAD_DIM]
            if m == 2:
                k = jnp.concatenate([keys[:, at], edge_qkv[1, :, at]], axis=0)
                grad = local_v[:, at].astype(f32) + jnp.where(after, nn(k, state), 0.0)
            else:
                v = jnp.concatenate([values[:, at], edge_qkv[2, :, at]], axis=0)
                slopes = jnp.concatenate([slope[:, at], edge_slope[:, at]], axis=0)
                grad = (local_k[:, at].astype(f32) + jnp.where(after, nt(v, state), 0.0)) * slopes
            out = conv_back(grad, taps.at[:, :, at], m, starts, first, rows)
            sent[:, m + 1, :, at] = out.reshape(shape)
    copy.wait()


def closed(starts, rows, i):
    found = jnp.bool_(False)
    for d in range(starts.shape[0]):
        found = found | ((starts[d] >= i * rows) & (starts[d] < (i + 1) * rows))
    return found


def forward_kernel(rows, starts, sums, out):
    count = sums.shape[0]
    state = jnp.zeros((SHARE, HEAD_DIM), f32)
    for i in range(count):
        here = sums[i].astype(f32)
        edge = sums[min(i + 1, count - 1)].astype(f32)[SHARE:]
        if i == count - 1:
            edge = jnp.zeros_like(edge)
        out[i] = jnp.concatenate([state, edge], axis=0).astype(bf16)
        state = here[:SHARE] + jnp.where(closed(starts, rows, i), 0.0, state)


def backward_kernel(rows, starts, sums, out):
    count = 2 * sums.shape[0]
    state = jnp.zeros((SHARE, HEAD_DIM), f32)
    for i in range(count - 1, 0, -2):
        pair = sums[i // 2].astype(f32)
        upper = state
        state = pair[SHARE:] + jnp.where(closed(starts, rows, i), 0.0, state)
        out[i // 2] = jnp.concatenate([state, upper], axis=0).astype(bf16)
        state = pair[:SHARE] + jnp.where(closed(starts, rows, i - 1), 0.0, state)


def gather_kernel(sent, out, grad):
    count, _, _, width = sent.shape
    for i in range(count):
        columns = slice(i * width, (i + 1) * width)
        out[:, columns] = sent[i, 0]
        for m in range(3):
            grad[m, :, columns] = sent[i, m + 1]


def shards(qkv_raw, conv_weight, norm_gain, doc_starts, cotangent):
    rows = qkv_raw.shape[0]
    width = qkv_raw.shape[2]
    heads = width // HEAD_DIM
    total = rows + HALO
    devices = lax.axis_size("seq")
    columns = lax.axis_size("head")
    piece = rows // columns
    share = devices // heads
    raw = qkv_raw.transpose(1, 0, 2)
    in_hbm = functools.partial(pltpu.with_memory_space_constraint, memory_space=pltpu.HBM)
    doc_starts = pltpu.with_memory_space_constraint(doc_starts, pltpu.SMEM)
    hd = HEAD_DIM

    ahead = [(i, i + 1) for i in range(devices - 1)]
    rim = lax.ppermute(raw[:, rows - HALO :], "seq", ahead)

    smem = pl.BlockSpec(memory_space=pltpu.SMEM)
    params = pltpu.CompilerParams(vmem_limit_bytes=16 * 1024 * 1024)

    vmem = pl.BlockSpec(memory_space=pltpu.VMEM)
    hbm = pl.BlockSpec(memory_space=pltpu.HBM)
    dma = pltpu.SemaphoreType.DMA

    def flat_call(body, ins, outs, scratch, *args, alias={}):
        return pl.pallas_call(
            body,
            in_specs=[smem] + ins,
            out_specs=[hbm if out.memory_space == pltpu.HBM else vmem for out in outs],
            out_shape=outs,
            scratch_shapes=scratch,
            input_output_aliases=alias,
            compiler_params=params,
        )(doc_starts, *[in_hbm(a) if spec is hbm else a for a, spec in zip(args, ins)])

    wide = pltpu.VMEM((rows, width), bf16)
    fetched = flat_call(
        fetch_kernel,
        [hbm] * 4,
        [
            pltpu.VMEM(raw.shape, bf16), pltpu.VMEM((3, HALO, width), bf16),
            pltpu.VMEM((4, HALO, width), bf16), pltpu.VMEM(conv_weight.shape, f32),
            pltpu.VMEM((1, width), f32),
        ],
        [dma((6,))],
        raw, cotangent, conv_weight, norm_gain.reshape(1, width),
    )
    rim, fetched = lax.optimization_barrier((rim, fetched))
    near, raw_end, tops, taps, gain = fetched
    keys, values, message = flat_call(
        conv_kernel,
        [vmem] * 4,
        [wide, wide, pltpu.VMEM((devices, 2 * SHARE, hd), bf16)],
        [],
        near, rim, tops, taps,
    )

    def swap(parts):
        return lax.all_to_all(parts, "seq", 0, 0, tiled=True)

    def scan(body, parts):
        (found,) = flat_call(
            functools.partial(body, rows), [vmem], [pltpu.VMEM(parts.shape, bf16)], [], parts
        )
        return found

    queries, local = flat_call(
        local_kernel, [vmem] * 5, [wide, pltpu.VMEM((rows, width), f32)], [],
        near, rim, taps, keys, values,
    )
    slope_q, slope_k = flat_call(
        slope_kernel, [vmem] * 3, [pltpu.VMEM((rows, width), f32)] * 2, [],
        near, rim, taps,
    )
    message, queries, local, slope_q, slope_k = lax.optimization_barrier(
        (swap(message), queries, local, slope_q, slope_k)
    )
    message = scan(forward_kernel, message)
    incoming = swap(message)
    attn_out, grad_norm, back = flat_call(
        norm_kernel,
        [vmem] * 5,
        [
            pltpu.VMEM((columns, piece, width), bf16), pltpu.VMEM((rows, width), bf16),
            pltpu.VMEM((heads * hd, hd), bf16),
        ],
        [],
        queries, local, incoming, cotangent, gain,
    )
    early, edge_qkv, edge_slope, edge_grad = flat_call(
        query_kernel,
        [vmem] * 9,
        [
            pltpu.VMEM((columns, 2, piece, width), bf16), pltpu.VMEM((3, HALO, width), bf16),
            pltpu.VMEM((HALO, width), f32), pltpu.VMEM((HALO, width), bf16),
        ],
        [dma(())],
        keys, values, grad_norm, slope_q, incoming, raw_end, taps, gain, attn_out,
    )
    back = swap(back.reshape(devices, SHARE, hd))
    back, early, edge_qkv, edge_slope, edge_grad = lax.optimization_barrier(
        (back, early, edge_qkv, edge_slope, edge_grad)
    )
    back = scan(backward_kernel, back.reshape(devices // 2, 2 * SHARE, hd))
    local_k, local_v = flat_call(
        key_kernel, [vmem] * 6, [pltpu.VMEM((total, width), bf16)] * 2, [],
        queries, keys, values, grad_norm, edge_qkv, edge_grad,
    )
    future, local_k, local_v = lax.optimization_barrier((swap(back.reshape(devices, SHARE, hd)), local_k, local_v))
    (sent,) = flat_call(
        last_kernel, [vmem] * 10, [pltpu.VMEM((columns, 4, piece, width), bf16)], [dma(())],
        keys, values, edge_qkv, slope_k, edge_slope, local_k, local_v,
        future.reshape(heads * hd, hd), taps, early,
    )
    sent = lax.all_to_all(sent, "head", 0, 0, tiled=True)
    out, grad = pl.pallas_call(
        gather_kernel,
        out_shape=[
            jax.ShapeDtypeStruct((piece, columns * width), bf16),
            jax.ShapeDtypeStruct((3, piece, columns * width), bf16),
        ],
        compiler_params=params,
    )(sent)
    return out, grad.transpose(1, 0, 2)


def solution(mesh):
    return jax.shard_map(
        shards,
        mesh=mesh,
        in_specs=(P("seq", None, "head"), P(None, None, "head"), P("head"), P(), P("seq", "head")),
        out_specs=(P(("seq", "head"), None), P(("seq", "head"), None, None)),
        check_vma=False,
    )
```

```python
import functools

import jax
import jax.numpy as jnp
from jax import lax
from jax.experimental import pallas as pl
from jax.experimental.pallas import tpu as pltpu
from jax.sharding import PartitionSpec as P

HEAD_DIM = 128
TAPS = 4
CHUNK = 128
HALO = 16
EDGE = TAPS - 1
ROUTE = 2 * EDGE
SHARE = 8
FAR = 1 << 30

f32 = jnp.float32
bf16 = jnp.bfloat16


def nt(a, b):
    return lax.dot_general(a, b, (((1,), (1,)), ((), ())), preferred_element_type=f32)


def nn(a, b):
    return lax.dot_general(a, b, (((1,), (0,)), ((), ())), preferred_element_type=f32)


def tn(a, b):
    return lax.dot_general(a, b, (((0,), (0,)), ((), ())), preferred_element_type=f32)


def doc_start(starts, first, pos):
    found = jnp.int32(-FAR)
    for d in range(starts.shape[0]):
        rel = starts[d] - first
        found = jnp.maximum(found, jnp.where(rel <= pos, rel, -FAR))
    return found


def doc_end(starts, first, pos):
    found = jnp.int32(FAR)
    for d in range(starts.shape[0]):
        rel = starts[d] - first
        found = jnp.minimum(found, jnp.where(rel > pos, rel, FAR))
    return found


def row_starts(starts, first, rows):
    found = jnp.full(rows.shape, -FAR, jnp.int32)
    for d in range(starts.shape[0]):
        rel = starts[d] - first
        found = jnp.maximum(found, jnp.where(rows >= rel, rel, -FAR))
    return found


def iota(shape, axis, base=0):
    return lax.broadcasted_iota(jnp.int32, shape, axis) + base


def conv_rows(ext, taps, m, age):
    conv = taps[m, 0:1] * ext
    for j in range(1, TAPS):
        conv = conv + jnp.where(age >= j, taps[m, j : j + 1] * pltpu.roll(ext, j, 0), 0.0)
    return conv


def logistic(x):
    return 1.0 / (1.0 + jnp.exp(-x))


def silu_slope(conv, sigma):
    return sigma * (1.0 + conv * (1.0 - sigma))


def conv_docs(ext, taps, m, starts, first):
    rows = ext.shape[0] - HALO
    conv = taps[m, 0:1] * ext
    for j in range(1, TAPS):
        conv = conv + taps[m, j : j + 1] * pltpu.roll(ext, j, 0)
    parts = []
    for low in range(0, rows, CHUNK):
        top = ext[HALO + low - SHARE : HALO + low + SHARE]
        age = iota((2 * SHARE, HEAD_DIM), 0, low - SHARE) - doc_start(starts, first, low)
        parts.append(conv_rows(top, taps, m, age)[SHARE:])
        parts.append(conv[HALO + low + SHARE : HALO + low + CHUNK])
    return jnp.concatenate(parts, axis=0)


def behind_mask(scores, begin):
    size, high = scores.shape
    parts = [
        jnp.where(at >= begin, scores[:, at : at + size], 0.0) for at in range(0, high - size, size)
    ]
    causal = iota((size, size), 1) <= iota((size, size), 0)
    parts.append(jnp.where(causal, scores[:, high - size :], 0.0))
    return jnp.concatenate(parts, axis=1).astype(bf16)


def ahead_mask(scores, low, end):
    size, length = scores.shape
    causal = iota((size, size), 1) >= iota((size, size), 0)
    parts = [jnp.where(causal, scores[:, :size], 0.0)]
    for at in range(size, length, size):
        parts.append(jnp.where(low + at < end, scores[:, at : at + size], 0.0))
    return jnp.concatenate(parts, axis=1).astype(bf16)


def head_columns(h):
    return slice(h * HEAD_DIM, (h + 1) * HEAD_DIM)


def spread(row):
    return jnp.broadcast_to(row, (SHARE, HEAD_DIM))


def only_top(block):
    return jnp.where(iota(block.shape, 0) < EDGE, block, jnp.zeros((), block.dtype))


def conv_kernel(
    starts, raw_far, cot_far, taps_far, gain_far,
    keys, values, slope_k, message, raw_q, raw_end, tops, taps, gain, raw, sems,
):
    _, rows, width = raw.shape
    heads = range(width // HEAD_DIM)
    first = lax.axis_index("seq") * rows
    taps_load = pltpu.make_async_copy(taps_far, taps, sems.at[0])
    loads = [pltpu.make_async_copy(raw_far.at[m], raw.at[m - 1], sems.at[m]) for m in (1, 2)]
    others = [
        pltpu.make_async_copy(raw_far.at[:, pl.ds(0, HALO)], tops.at[pl.ds(0, 3)], sems.at[3]),
        pltpu.make_async_copy(cot_far.at[pl.ds(0, HALO)], tops.at[3], sems.at[4]),
        pltpu.make_async_copy(raw_far.at[:, pl.ds(rows - HALO, HALO)], raw_end, sems.at[5]),
        pltpu.make_async_copy(raw_far.at[0], raw_q, sems.at[6]),
        pltpu.make_async_copy(gain_far, gain, sems.at[7]),
    ]
    for load in [loads[0], taps_load, loads[1]] + others:
        load.start()
    taps_load.wait()
    begin = jnp.maximum(doc_start(starts, first, rows - 1), EDGE)
    keep = iota((rows, HEAD_DIM), 0) >= begin
    made = {}
    for m, out in ((1, keys), (2, values)):
        loads[m - 1].wait()
        for h in heads:
            at = head_columns(h)
            ext = jnp.concatenate(
                [jnp.zeros((HALO, HEAD_DIM), f32), raw[m - 1, :, at].astype(f32)], axis=0
            )
            conv = conv_docs(ext, taps.at[:, :, at], m, starts, first)
            if m == 1:
                sigma = logistic(conv)
                slope_k[:, at] = silu_slope(conv, sigma)
                conv = conv * sigma
            made[m, h] = conv.astype(bf16)
            out[:, at] = made[m, h]
    for load in others:
        load.wait()
    share = HEAD_DIM // SHARE
    line = iota((SHARE, HEAD_DIM), 0)
    ends, routed = {}, []
    for h in heads:
        at = head_columns(h)
        for m in range(3):
            low = raw_end[m, :, at].astype(f32)[HALO - SHARE :]
            top = tops[m, :, at].astype(f32)[:SHARE]
            ends[m, h] = pltpu.roll(jnp.where(line >= SHARE - EDGE, low, top), EDGE, 0)
    for base in (0, EDGE):
        for h in heads:
            routed += [ends[0, h][base + a : base + a + 1] for a in range(EDGE)]
    for h in heads:
        top = tops[3, :, head_columns(h)].astype(f32)
        routed += [top[a : a + 1] for a in range(EDGE)]
    for h in heads:
        summary = tn(jnp.where(keep, made[1, h], jnp.zeros((), bf16)), made[2, h])
        for n in range(share):
            r = h * share + n
            k_ends = ends[1, h]
            if r < len(routed):
                k_ends = jnp.where(line == ROUTE, spread(routed[r]), k_ends)
            part = summary[n * SHARE : (n + 1) * SHARE]
            message[r] = jnp.concatenate([part, k_ends, ends[2, h]], axis=0).astype(bf16)


def local_kernel(starts, raw_q, taps, keys, values, queries, slope_q, local):
    rows, width = local.shape
    first = lax.axis_index("seq") * rows
    for h in range(width // HEAD_DIM):
        at = head_columns(h)
        ext = jnp.concatenate(
            [jnp.zeros((HALO, HEAD_DIM), f32), raw_q[:, at].astype(f32)], axis=0
        )
        conv = conv_docs(ext, taps.at[:, :, at], 0, starts, first)
        sigma = logistic(conv)
        slope_q[:, at] = silu_slope(conv, sigma)
        q = (conv * sigma).astype(bf16)
        queries[:, at] = q
        for low in range(0, rows, CHUNK):
            high = low + CHUNK
            start = doc_start(starts, first, low)
            scores = behind_mask(nt(q[low:high], keys[:high, at]), start)
            scores = jnp.where(iota(scores.shape, 1) >= EDGE, scores, jnp.zeros((), bf16))
            local[low:high, at] = nn(scores, values[:high, at])


def state_of(message):
    return message.astype(f32)[:, :SHARE].reshape(HEAD_DIM, HEAD_DIM)


def heard_ends(incoming, m, h, heads):
    share = HEAD_DIM // SHARE
    if m:
        return incoming[h * share + m - 1].astype(f32)[SHARE:]
    line = iota((SHARE, HEAD_DIM), 0)
    block = jnp.zeros((SHARE, HEAD_DIM), f32)
    for a in range(2 * EDGE):
        r = (a // EDGE * heads + h) * EDGE + a % EDGE
        row = incoming[r].astype(f32)[SHARE + ROUTE : SHARE + ROUTE + 1]
        block = jnp.where(line == a, spread(row), block)
    return block


def next_cot(incoming, h, heads):
    line = iota((SHARE, HEAD_DIM), 0)
    block = jnp.zeros((SHARE, HEAD_DIM), f32)
    for a in range(EDGE):
        r = (2 * heads + h) * EDGE + a
        row = incoming[r].astype(f32)[SHARE + ROUTE : SHARE + ROUTE + 1]
        block = jnp.where(line == a, spread(row), block)
    return block


def to_halo(block):
    return jnp.concatenate([block, jnp.zeros((HALO - SHARE, HEAD_DIM), block.dtype)], axis=0)


def patched(top, column):
    return jnp.concatenate([top, column[top.shape[0] :]], axis=0)


def normed(attn, gains, cots):
    msq = jnp.mean(attn * attn, axis=-1, keepdims=True)
    scale = lax.rsqrt(jnp.maximum(msq, 1.0))
    scaled = cots * gains
    inner = jnp.mean(scaled * attn, axis=-1, keepdims=True)
    factor = jnp.where(msq > 1.0, scale * scale * scale * inner, 0.0)
    return scale, (scale * scaled - attn * factor).astype(bf16)


def norm_kernel(
    starts, queries, local, incoming, cot, gain, tops, taps, slope_q, slope_k, keys, values,
    attn_out, grad_norm, back, top_qkv, top_slope,
):
    rows, width = local.shape
    heads = width // HEAD_DIM
    share = HEAD_DIM // SHARE
    first = lax.axis_index("seq") * rows
    begin = row_starts(starts, first, iota((rows, HEAD_DIM), 0))
    joined = doc_start(starts, first, 0) < 0
    line = iota((SHARE, HEAD_DIM), 0)
    causal = iota((HALO, HALO), 1) <= iota((HALO, HALO), 0)
    for h in range(heads):
        at = head_columns(h)
        top = []
        for m, made in enumerate((queries, keys, values)):
            behind = jnp.where(joined, heard_ends(incoming, m, h, heads), 0.0)
            own = pltpu.roll(tops[m, :, at].astype(f32)[:SHARE], EDGE, 0)
            ext = jnp.where(line < EDGE, behind, own)
            conv = taps[m, 0:1, at] * ext
            for j in range(1, TAPS):
                conv = conv + taps[m, j : j + 1, at] * pltpu.roll(ext, j, 0)
            conv = pltpu.roll(conv, SHARE - EDGE, 0)
            if m < 2:
                sigma = logistic(conv)
                old = (slope_q, slope_k)[m][:SHARE, at]
                top_slope[m, :, at] = jnp.where(line < EDGE, silu_slope(conv, sigma), old)
                conv = conv * sigma
            fresh = to_halo(only_top(conv)).astype(bf16)
            top.append(fresh)
            old = made[:HALO, at]
            top_qkv[m, :, at] = jnp.where(iota((HALO, HEAD_DIM), 0) < EDGE, fresh, old)
        q_top, k_top, v_top = top
        state = jnp.where(joined, state_of(incoming[h * share : (h + 1) * share]), 0.0)
        carried = nn(queries[:, at], (state + tn(k_top, v_top)).astype(bf16))
        attn = local[:, at] + jnp.where(begin <= 0, carried, 0.0)
        scores = jnp.where(causal, nt(q_top, k_top), 0.0).astype(bf16)
        attn_top = nn(scores, v_top) + nn(q_top, state.astype(bf16))
        attn = patched(jnp.where(line < EDGE, attn_top[:SHARE], attn[:SHARE]), attn)
        scale, grad = normed(attn, gain[:, at], cot[:, at].astype(f32))
        out = (attn * scale * gain[:, at]).astype(bf16)
        attn_out[:, :, at] = out.reshape(attn_out.shape[:2] + (HEAD_DIM,))
        grad_norm[:, at] = grad
        q = patched(top_qkv[0, :, at], queries[:, at])
        masked_q = jnp.where(begin < 0, q, jnp.zeros((), bf16))
        back[h * HEAD_DIM : (h + 1) * HEAD_DIM] = tn(masked_q, grad).astype(bf16)


def conv_back(grad, taps, m, starts, first, rows):
    total = grad.shape[0]
    out = taps[m, 0:1] * grad[:rows]
    for j in range(1, TAPS):
        out = out + pltpu.roll(taps[m, j : j + 1] * grad, total - j, 0)[:rows]
    parts = []
    for high in range(CHUNK, rows + 1, CHUNK):
        near = grad[high - SHARE : high + SHARE]
        age = iota((2 * SHARE, HEAD_DIM), 0, high - SHARE)
        age = age - row_starts(starts, first, age)
        end = taps[m, 0:1] * near[:SHARE]
        for j in range(1, TAPS):
            term = jnp.where(age >= j, taps[m, j : j + 1] * near, 0.0)
            end = end + pltpu.roll(term, 2 * SHARE - j, 0)[:SHARE]
        parts.append(out[high - CHUNK : high - SHARE])
        parts.append(end)
    return jnp.concatenate(parts, axis=0).astype(bf16)


def query_kernel(
    starts, keys, values, top_qkv, top_slope, grad_norm, slope, incoming, raw_end, taps, gain,
    attn_out, early, edge_qkv, edge_slope, edge_grad, sem,
):
    rows, width = grad_norm.shape
    heads = width // HEAD_DIM
    share = HEAD_DIM // SHARE
    first = lax.axis_index("seq") * rows
    copy = pltpu.make_async_copy(attn_out, early.at[:, 0], sem)
    copy.start()
    carry = row_starts(starts, first, iota((rows, HEAD_DIM), 0)) < 0
    start = doc_start(starts, first, rows)
    edge_age = iota((2 * HALO, HEAD_DIM), 0, rows - HALO)
    edge_age = edge_age - row_starts(starts, first, edge_age)
    reach = iota((HALO, rows), 1) >= start
    causal = iota((HALO, HALO), 1) <= iota((HALO, HALO), 0)
    for h in range(heads):
        at = head_columns(h)
        state = state_of(incoming[h * share : (h + 1) * share]).astype(bf16)
        k = patched(top_qkv[1, :, at], keys[:, at])
        v = patched(top_qkv[2, :, at], values[:, at])
        g = grad_norm[:, at]
        slope_top = patched(top_slope[0, :, at], slope[:, at])
        edges, slopes = [], []
        for m in range(3):
            after = pltpu.roll(heard_ends(incoming, m, h, heads), SHARE - EDGE, 0)
            after = to_halo(only_top(after))
            ext = jnp.concatenate([raw_end[m, :, at].astype(f32), after], axis=0)
            conv = conv_rows(ext, taps.at[:, :, at], m, edge_age)[HALO:]
            if m < 2:
                sigma = logistic(conv)
                slopes.append(silu_slope(conv, sigma))
                conv = conv * sigma
            edges.append(conv.astype(bf16))
            edge_qkv[m, :, at] = edges[m]
        edge_slope[:, at] = slopes[1]
        q_e, k_e, v_e = edges

        def edge_sums(left, right, right_e, values, values_e, carried):
            scores = jnp.where(reach, nt(left, right), 0.0).astype(bf16)
            scores_e = jnp.where(causal, nt(left, right_e), 0.0).astype(bf16)
            added = jnp.where(start < 0, carried, 0.0)
            return nn(scores, values) + nn(scores_e, values_e) + added

        attn_e = edge_sums(q_e, k, k_e, v, v_e, nn(q_e, state))
        _, g_e = normed(attn_e, gain[:, at], to_halo(next_cot(incoming, h, heads)))
        edge_grad[:, at] = g_e
        grad_q_e = edge_sums(g_e, v, v_e, k, k_e, nt(g_e, state)) * slopes[0]

        parts = []
        for low in range(0, rows, CHUNK):
            high = low + CHUNK
            begin = doc_start(starts, first, low)
            parts.append(nn(behind_mask(nt(g[low:high], v[:high]), begin), k[:high]))
        carried = jnp.where(carry, nt(g, state), 0.0)
        grad_q = (jnp.concatenate(parts, axis=0) + carried) * slope_top
        both = jnp.concatenate([grad_q, grad_q_e], axis=0)
        out = conv_back(both, taps.at[:, :, at], 0, starts, first, rows)
        early[:, 1, :, at] = out.reshape((early.shape[0], early.shape[2], HEAD_DIM))
    copy.wait()


def key_kernel(
    starts, queries, keys, values, top_qkv, grad_norm, edge_qkv, edge_grad, local_k, local_v
):
    rows, width = grad_norm.shape
    first = lax.axis_index("seq") * rows
    for h in range(width // HEAD_DIM):
        at = head_columns(h)
        columns = (queries[:, at], keys[:, at], values[:, at])
        q, k, v = [patched(top_qkv[m, :, at], columns[m]) for m in range(3)]
        g = grad_norm[:, at]
        for low in range(0, rows, CHUNK):
            high = low + CHUNK
            end = doc_end(starts, first, low)
            scores = ahead_mask(nt(v[low:high], g[low:]), low, end)
            local_k[low:high, at] = nn(scores, q[low:]).astype(bf16)
            scores = ahead_mask(nt(k[low:high], q[low:]), low, end)
            local_v[low:high, at] = nn(scores, g[low:]).astype(bf16)
        q_e, k_e, v_e = edge_qkv[0, :, at], edge_qkv[1, :, at], edge_qkv[2, :, at]
        g_e = edge_grad[:, at]
        earlier = iota((HALO, HALO), 1) < iota((HALO, HALO), 0)
        scores = jnp.where(earlier, -nt(v_e, g_e), 0.0).astype(bf16)
        local_k[rows:, at] = nn(scores, q_e).astype(bf16)
        scores = jnp.where(earlier, -nt(k_e, q_e), 0.0).astype(bf16)
        local_v[rows:, at] = nn(scores, g_e).astype(bf16)


def last_kernel(
    starts, keys, values, top_qkv, top_slope, edge_qkv, slope, edge_slope, local_k, local_v,
    future, taps, early, sent, sem,
):
    total, width = local_k.shape
    rows = total - HALO
    first = lax.axis_index("seq") * rows
    copy = pltpu.make_async_copy(early, sent.at[:, pl.ds(0, 2)], sem)
    copy.start()
    after = iota((total, HEAD_DIM), 0) >= doc_start(starts, first, rows)
    shape = (sent.shape[0], sent.shape[2], HEAD_DIM)
    for m in (2, 1):
        for h in range(width // HEAD_DIM):
            at = head_columns(h)
            state = future[h * HEAD_DIM : (h + 1) * HEAD_DIM]
            if m == 2:
                k = patched(top_qkv[1, :, at], keys[:, at])
                k = jnp.concatenate([k, edge_qkv[1, :, at]], axis=0)
                grad = local_v[:, at].astype(f32) + jnp.where(after, nn(k, state), 0.0)
            else:
                v = patched(top_qkv[2, :, at], values[:, at])
                v = jnp.concatenate([v, edge_qkv[2, :, at]], axis=0)
                slopes = patched(top_slope[1, :, at], slope[:, at])
                slopes = jnp.concatenate([slopes, edge_slope[:, at]], axis=0)
                grad = (local_k[:, at].astype(f32) + jnp.where(after, nt(v, state), 0.0)) * slopes
            out = conv_back(grad, taps.at[:, :, at], m, starts, first, rows)
            sent[:, m + 1, :, at] = out.reshape(shape)
    copy.wait()


def closed(starts, rows, i):
    found = jnp.bool_(False)
    for d in range(starts.shape[0]):
        found = found | ((starts[d] >= i * rows) & (starts[d] < (i + 1) * rows))
    return found


def forward_kernel(rows, starts, sums, taps, out):
    count = sums.shape[0]
    share = HEAD_DIM // SHARE
    place = lax.axis_index("seq")
    part, head = lax.rem(place, share), lax.div(place, share)
    line = iota((SHARE, HEAD_DIM), 0)
    inside = (line >= EDGE) & (line < 2 * EDGE)
    nothing = jnp.zeros((SHARE, HEAD_DIM), f32)

    def tap(m, j):
        row = taps[m, j : j + 1, :HEAD_DIM]
        for h in range(1, taps.shape[2] // HEAD_DIM):
            row = jnp.where(head == h, taps[m, j : j + 1, head_columns(h)], row)
        return row

    heard = [sums[i].astype(f32) for i in range(count)]
    ends = {m: [block[m * SHARE : (m + 1) * SHARE] for block in heard] for m in (1, 2)}
    tops = {1: [], 2: []}
    for m in (1, 2):
        weights = [tap(m, j) for j in range(TAPS)]
        for i in range(count):
            begun, split = jnp.bool_(False), jnp.bool_(False)
            for d in range(starts.shape[0]):
                begun = begun | (starts[d] == i * rows)
                split = split | ((starts[d] > i * rows) & (starts[d] < (i + 1) * rows))
            behind = jnp.where(begun, 0.0, ends[m][i - 1]) if i else nothing
            ext = jnp.where(line < EDGE, behind, ends[m][i])
            conv = weights[0] * ext
            for j in range(1, TAPS):
                conv = conv + weights[j] * pltpu.roll(ext, j, 0)
            if m == 1:
                conv = jnp.where(split, 0.0, conv * logistic(conv))
            tops[m].append(jnp.where(inside, conv, 0.0))
    k_tops, v_tops = [jnp.concatenate(tops[m], axis=0).astype(bf16) for m in (1, 2)]
    own = iota((SHARE, HEAD_DIM), 1) == line + part * SHARE
    picked = nt(jnp.where(own, 1.0, 0.0).astype(bf16), k_tops)
    size = count * SHARE
    same = lax.div(iota((size, size), 0), SHARE) == lax.div(iota((size, size), 1), SHARE)
    picked = jnp.where(same, jnp.concatenate([picked] * count, axis=0), 0.0).astype(bf16)
    added = nn(picked, v_tops)
    state = nothing
    for i in range(count):
        sides = []
        for j in (i - 1, i + 1):
            if 0 <= j < count:
                sides.append((jnp.where(lax.rem(part, 2) == 0, ends[1][j], ends[2][j]), ends[1][j]))
            else:
                sides.append((nothing, nothing))
        block = jnp.where(line < EDGE, sides[0][0], sides[1][0])
        route = jnp.where(place < EDGE * (taps.shape[2] // HEAD_DIM), sides[0][1], sides[1][1])
        block = jnp.where(line == ROUTE, route, block)
        out[i] = jnp.concatenate([state, block], axis=0).astype(bf16)
        new = heard[i][:SHARE] + added[i * SHARE : (i + 1) * SHARE]
        state = new + jnp.where(closed(starts, rows, i), 0.0, state)


def backward_kernel(rows, starts, sums, out):
    count = 2 * sums.shape[0]
    state = jnp.zeros((SHARE, HEAD_DIM), f32)
    for i in range(count - 1, 0, -2):
        pair = sums[i // 2].astype(f32)
        upper = state
        state = pair[SHARE:] + jnp.where(closed(starts, rows, i), 0.0, state)
        out[i // 2] = jnp.concatenate([state, upper], axis=0).astype(bf16)
        state = pair[:SHARE] + jnp.where(closed(starts, rows, i - 1), 0.0, state)


def gather_kernel(sent, out, grad):
    count, _, _, width = sent.shape
    for i in range(count):
        columns = slice(i * width, (i + 1) * width)
        out[:, columns] = sent[i, 0]
        for m in range(3):
            grad[m, :, columns] = sent[i, m + 1]


def shards(qkv_raw, conv_weight, norm_gain, doc_starts, cotangent):
    rows = qkv_raw.shape[0]
    width = qkv_raw.shape[2]
    heads = width // HEAD_DIM
    total = rows + HALO
    devices = lax.axis_size("seq")
    columns = lax.axis_size("head")
    piece = rows // columns
    share = devices // heads
    raw = qkv_raw.transpose(1, 0, 2)
    in_hbm = functools.partial(pltpu.with_memory_space_constraint, memory_space=pltpu.HBM)
    doc_starts = pltpu.with_memory_space_constraint(doc_starts, pltpu.SMEM)
    hd = HEAD_DIM


    smem = pl.BlockSpec(memory_space=pltpu.SMEM)
    params = pltpu.CompilerParams(vmem_limit_bytes=16 * 1024 * 1024)

    vmem = pl.BlockSpec(memory_space=pltpu.VMEM)
    hbm = pl.BlockSpec(memory_space=pltpu.HBM)
    dma = pltpu.SemaphoreType.DMA

    def flat_call(body, ins, outs, scratch, *args, alias={}):
        return pl.pallas_call(
            body,
            in_specs=[smem] + ins,
            out_specs=[hbm if out.memory_space == pltpu.HBM else vmem for out in outs],
            out_shape=outs,
            scratch_shapes=scratch,
            input_output_aliases=alias,
            compiler_params=params,
        )(doc_starts, *[in_hbm(a) if spec is hbm else a for a, spec in zip(args, ins)])

    wide = pltpu.VMEM((rows, width), bf16)
    tall = pltpu.VMEM((rows, width), f32)
    keys, values, slope_k, message, raw_q, raw_end, tops, taps, gain = flat_call(
        conv_kernel,
        [hbm] * 4,
        [
            wide, wide, tall, pltpu.VMEM((devices, 3 * SHARE, hd), bf16), wide,
            pltpu.VMEM((3, HALO, width), bf16), pltpu.VMEM((4, HALO, width), bf16),
            pltpu.VMEM(conv_weight.shape, f32), pltpu.VMEM((1, width), f32),
        ],
        [pltpu.VMEM((2, rows, width), bf16), dma((8,))],
        raw, cotangent, conv_weight, norm_gain.reshape(1, width),
    )

    def swap(parts):
        return lax.all_to_all(parts, "seq", 0, 0, tiled=True)

    def scan(body, shape, parts, *others):
        (found,) = flat_call(
            functools.partial(body, rows), [vmem] * (1 + len(others)),
            [pltpu.VMEM(shape, bf16)], [], parts, *others,
        )
        return found

    queries, slope_q, local = flat_call(
        local_kernel, [vmem] * 4, [wide, tall, tall], [],
        raw_q, taps, keys, values,
    )
    message, queries, slope_q, local = lax.optimization_barrier(
        (swap(message), queries, slope_q, local)
    )
    message = scan(forward_kernel, (devices, 2 * SHARE, hd), message, taps)
    incoming = swap(message)
    attn_out, grad_norm, back, top_qkv, top_slope = flat_call(
        norm_kernel,
        [vmem] * 11,
        [
            pltpu.VMEM((columns, piece, width), bf16), wide,
            pltpu.VMEM((heads * hd, hd), bf16), pltpu.VMEM((3, HALO, width), bf16),
            pltpu.VMEM((2, SHARE, width), f32),
        ],
        [],
        queries, local, incoming, cotangent, gain, tops, taps, slope_q, slope_k, keys, values,
    )
    early, edge_qkv, edge_slope, edge_grad = flat_call(
        query_kernel,
        [vmem] * 11,
        [
            pltpu.VMEM((columns, 2, piece, width), bf16), pltpu.VMEM((3, HALO, width), bf16),
            pltpu.VMEM((HALO, width), f32), pltpu.VMEM((HALO, width), bf16),
        ],
        [dma(())],
        keys, values, top_qkv, top_slope, grad_norm, slope_q, incoming, raw_end, taps, gain,
        attn_out,
    )
    back = swap(back.reshape(devices, SHARE, hd))
    back, early, edge_qkv, edge_slope, edge_grad = lax.optimization_barrier(
        (back, early, edge_qkv, edge_slope, edge_grad)
    )
    pairs = (devices // 2, 2 * SHARE, hd)
    back = scan(backward_kernel, pairs, back.reshape(pairs))
    local_k, local_v = flat_call(
        key_kernel, [vmem] * 7, [pltpu.VMEM((total, width), bf16)] * 2, [],
        queries, keys, values, top_qkv, grad_norm, edge_qkv, edge_grad,
    )
    future, local_k, local_v = lax.optimization_barrier((swap(back.reshape(devices, SHARE, hd)), local_k, local_v))
    (sent,) = flat_call(
        last_kernel, [vmem] * 12, [pltpu.VMEM((columns, 4, piece, width), bf16)], [dma(())],
        keys, values, top_qkv, top_slope, edge_qkv, slope_k, edge_slope, local_k, local_v,
        future.reshape(heads * hd, hd), taps, early,
    )
    sent = lax.all_to_all(sent, "head", 0, 0, tiled=True)
    out, grad = pl.pallas_call(
        gather_kernel,
        out_shape=[
            jax.ShapeDtypeStruct((piece, columns * width), bf16),
            jax.ShapeDtypeStruct((3, piece, columns * width), bf16),
        ],
        compiler_params=params,
    )(sent)
    return out, grad.transpose(1, 0, 2)


def solution(mesh):
    return jax.shard_map(
        shards,
        mesh=mesh,
        in_specs=(P("seq", None, "head"), P(None, None, "head"), P("head"), P(), P("seq", "head")),
        out_specs=(P(("seq", "head"), None), P(("seq", "head"), None, None)),
        check_vma=False,
    )
```

```python
import functools

import jax
import jax.numpy as jnp
from jax import lax
from jax.experimental import pallas as pl
from jax.experimental.pallas import tpu as pltpu
from jax.sharding import PartitionSpec as P

HEAD_DIM = 128
TAPS = 4
CHUNK = 128
SPAN = 256
HALO = 16
EDGE = TAPS - 1
ROUTE = 2 * EDGE
SHARE = 8
FAR = 1 << 30

f32 = jnp.float32
bf16 = jnp.bfloat16


def nt(a, b):
    return lax.dot_general(a, b, (((1,), (1,)), ((), ())), preferred_element_type=f32)


def nn(a, b):
    return lax.dot_general(a, b, (((1,), (0,)), ((), ())), preferred_element_type=f32)


def tn(a, b):
    return lax.dot_general(a, b, (((0,), (0,)), ((), ())), preferred_element_type=f32)


def doc_start(starts, first, pos):
    found = jnp.int32(-FAR)
    for d in range(starts.shape[0]):
        rel = starts[d] - first
        found = jnp.maximum(found, jnp.where(rel <= pos, rel, -FAR))
    return found


def doc_end(starts, first, pos):
    found = jnp.int32(FAR)
    for d in range(starts.shape[0]):
        rel = starts[d] - first
        found = jnp.minimum(found, jnp.where(rel > pos, rel, FAR))
    return found


def row_starts(starts, first, rows):
    found = jnp.full(rows.shape, -FAR, jnp.int32)
    for d in range(starts.shape[0]):
        rel = starts[d] - first
        found = jnp.maximum(found, jnp.where(rows >= rel, rel, -FAR))
    return found


def iota(shape, axis, base=0):
    return lax.broadcasted_iota(jnp.int32, shape, axis) + base


def conv_rows(ext, taps, m, age):
    conv = taps[m, 0:1] * ext
    for j in range(1, TAPS):
        conv = conv + jnp.where(age >= j, taps[m, j : j + 1] * pltpu.roll(ext, j, 0), 0.0)
    return conv


def logistic(x):
    return 1.0 / (1.0 + jnp.exp(-x))


def silu_slope(conv, sigma):
    return sigma * (1.0 + conv * (1.0 - sigma))


def conv_docs(ext, taps, m, starts, first):
    rows = ext.shape[0] - HALO
    conv = taps[m, 0:1] * ext
    for j in range(1, TAPS):
        conv = conv + taps[m, j : j + 1] * pltpu.roll(ext, j, 0)
    parts = []
    for low in range(0, rows, CHUNK):
        top = ext[HALO + low - SHARE : HALO + low + SHARE]
        age = iota((2 * SHARE, HEAD_DIM), 0, low - SHARE) - doc_start(starts, first, low)
        parts.append(conv_rows(top, taps, m, age)[SHARE:])
        parts.append(conv[HALO + low + SHARE : HALO + low + CHUNK])
    return jnp.concatenate(parts, axis=0)


def behind_mask(scores, low, starts, first, least=0):
    size, high = scores.shape
    causal = iota((CHUNK, CHUNK), 1) <= iota((CHUNK, CHUNK), 0)
    late = iota((CHUNK, CHUNK), 1) >= least
    bands = []
    for top in range(low, low + size, CHUNK):
        begin = doc_start(starts, first, top)
        parts = []
        for at in range(0, high, CHUNK):
            part = scores[top - low : top - low + CHUNK, at : at + CHUNK]
            if at > top:
                part = jnp.zeros_like(part)
            elif at == top:
                part = jnp.where(causal & late if at == 0 and least else causal, part, 0.0)
            else:
                part = jnp.where(at >= begin, part, 0.0)
                if at == 0 and least:
                    part = jnp.where(late, part, 0.0)
            parts.append(part)
        bands.append(jnp.concatenate(parts, axis=1))
    return jnp.concatenate(bands, axis=0).astype(bf16)


def ahead_mask(scores, low, starts, first):
    size, length = scores.shape
    causal = iota((CHUNK, CHUNK), 1) >= iota((CHUNK, CHUNK), 0)
    bands = []
    for top in range(low, low + size, CHUNK):
        end = doc_end(starts, first, top)
        parts = []
        for at in range(low, low + length, CHUNK):
            part = scores[top - low : top - low + CHUNK, at - low : at - low + CHUNK]
            if at < top:
                part = jnp.zeros_like(part)
            elif at == top:
                part = jnp.where(causal, part, 0.0)
            else:
                part = jnp.where(at < end, part, 0.0)
            parts.append(part)
        bands.append(jnp.concatenate(parts, axis=1))
    return jnp.concatenate(bands, axis=0).astype(bf16)


def head_columns(h):
    return slice(h * HEAD_DIM, (h + 1) * HEAD_DIM)


def spread(row):
    return jnp.broadcast_to(row, (SHARE, HEAD_DIM))


def only_top(block):
    return jnp.where(iota(block.shape, 0) < EDGE, block, jnp.zeros((), block.dtype))


def conv_kernel(
    starts_far, raw_far, cot_far, taps_far, gain_far,
    keys, values, message, raw_end, tops, taps, gain, raw, starts, sems,
):
    _, rows, width = raw.shape
    heads = range(width // HEAD_DIM)
    first = lax.axis_index("seq") * rows
    taps_load = pltpu.make_async_copy(taps_far, taps, sems.at[0])
    loads = [pltpu.make_async_copy(raw_far.at[m], raw.at[m - 1], sems.at[m]) for m in (1, 2)]
    others = [
        pltpu.make_async_copy(raw_far.at[:, pl.ds(0, HALO)], tops.at[pl.ds(0, 3)], sems.at[3]),
        pltpu.make_async_copy(cot_far.at[pl.ds(0, HALO)], tops.at[3], sems.at[4]),
        pltpu.make_async_copy(raw_far.at[:, pl.ds(rows - HALO, HALO)], raw_end, sems.at[5]),
        pltpu.make_async_copy(gain_far, gain, sems.at[6]),
    ]
    starts_load = pltpu.make_async_copy(starts_far, starts, sems.at[7])
    for load in [starts_load, loads[0], taps_load, loads[1]] + others:
        load.start()
    starts_load.wait()
    taps_load.wait()
    begin = jnp.maximum(doc_start(starts, first, rows - 1), EDGE)
    keep = iota((rows, HEAD_DIM), 0) >= begin
    made = {}
    for m, out in ((1, keys), (2, values)):
        loads[m - 1].wait()
        for h in heads:
            at = head_columns(h)
            ext = jnp.concatenate(
                [jnp.zeros((HALO, HEAD_DIM), f32), raw[m - 1, :, at].astype(f32)], axis=0
            )
            conv = conv_docs(ext, taps.at[:, :, at], m, starts, first)
            if m == 1:
                conv = conv * logistic(conv)
            made[m, h] = conv.astype(bf16)
            out[:, at] = made[m, h]
    for load in others:
        load.wait()
    share = HEAD_DIM // SHARE
    line = iota((SHARE, HEAD_DIM), 0)
    ends, routed = {}, []
    for h in heads:
        at = head_columns(h)
        for m in range(3):
            low = raw_end[m, :, at].astype(f32)[HALO - SHARE :]
            top = tops[m, :, at].astype(f32)[:SHARE]
            ends[m, h] = pltpu.roll(jnp.where(line >= SHARE - EDGE, low, top), EDGE, 0)
    for base in (0, EDGE):
        for h in heads:
            routed += [ends[0, h][base + a : base + a + 1] for a in range(EDGE)]
    for h in heads:
        top = tops[3, :, head_columns(h)].astype(f32)
        routed += [top[a : a + 1] for a in range(EDGE)]
    for h in heads:
        summary = tn(jnp.where(keep, made[1, h], jnp.zeros((), bf16)), made[2, h])
        for n in range(share):
            r = h * share + n
            k_ends = ends[1, h]
            if r < len(routed):
                k_ends = jnp.where(line == ROUTE, spread(routed[r]), k_ends)
            part = summary[n * SHARE : (n + 1) * SHARE]
            message[r] = jnp.concatenate([part, k_ends, ends[2, h]], axis=0).astype(bf16)


def local_kernel(
    starts, raw_far, taps, keys, values, queries, slope_q, slope_k, local, raw, sems
):
    rows, width = local.shape
    first = lax.axis_index("seq") * rows
    loads = [pltpu.make_async_copy(raw_far.at[m], raw.at[m], sems.at[m]) for m in range(2)]
    for load in loads:
        load.start()
    for m, slope in ((0, slope_q), (1, slope_k)):
        loads[m].wait()
        for h in range(width // HEAD_DIM):
            at = head_columns(h)
            ext = jnp.concatenate(
                [jnp.zeros((HALO, HEAD_DIM), f32), raw[m, :, at].astype(f32)], axis=0
            )
            conv = conv_docs(ext, taps.at[:, :, at], m, starts, first)
            sigma = logistic(conv)
            slope[:, at] = silu_slope(conv, sigma)
            if m == 0:
                queries[:, at] = (conv * sigma).astype(bf16)
    for h in range(width // HEAD_DIM):
        at = head_columns(h)
        for low in range(0, rows, SPAN):
            high = low + SPAN
            scores = nt(queries[low:high, at], keys[:high, at])
            scores = behind_mask(scores, low, starts, first, EDGE)
            local[low:high, at] = nn(scores, values[:high, at])


def state_of(message):
    return message.astype(f32)[:, :SHARE].reshape(HEAD_DIM, HEAD_DIM)


def heard_ends(incoming, m, h, heads):
    share = HEAD_DIM // SHARE
    if m:
        return incoming[h * share + m - 1].astype(f32)[SHARE:]
    line = iota((SHARE, HEAD_DIM), 0)
    block = jnp.zeros((SHARE, HEAD_DIM), f32)
    for a in range(2 * EDGE):
        r = (a // EDGE * heads + h) * EDGE + a % EDGE
        row = incoming[r].astype(f32)[SHARE + ROUTE : SHARE + ROUTE + 1]
        block = jnp.where(line == a, spread(row), block)
    return block


def next_cot(incoming, h, heads):
    line = iota((SHARE, HEAD_DIM), 0)
    block = jnp.zeros((SHARE, HEAD_DIM), f32)
    for a in range(EDGE):
        r = (2 * heads + h) * EDGE + a
        row = incoming[r].astype(f32)[SHARE + ROUTE : SHARE + ROUTE + 1]
        block = jnp.where(line == a, spread(row), block)
    return block


def to_halo(block):
    return jnp.concatenate([block, jnp.zeros((HALO - SHARE, HEAD_DIM), block.dtype)], axis=0)


def patched(top, column):
    return jnp.concatenate([top, column[top.shape[0] :]], axis=0)


def normed(attn, gains, cots):
    msq = jnp.mean(attn * attn, axis=-1, keepdims=True)
    scale = lax.rsqrt(jnp.maximum(msq, 1.0))
    scaled = cots * gains
    inner = jnp.mean(scaled * attn, axis=-1, keepdims=True)
    factor = jnp.where(msq > 1.0, scale * scale * scale * inner, 0.0)
    return scale, (scale * scaled - attn * factor).astype(bf16)


def norm_kernel(
    starts, queries, local, incoming, cot, gain, tops, taps, slope_q, slope_k, keys, values,
    attn_out, grad_norm, back, top_qkv, top_slope,
):
    rows, width = local.shape
    heads = width // HEAD_DIM
    share = HEAD_DIM // SHARE
    first = lax.axis_index("seq") * rows
    begin = row_starts(starts, first, iota((rows, HEAD_DIM), 0))
    joined = doc_start(starts, first, 0) < 0
    line = iota((SHARE, HEAD_DIM), 0)
    causal = iota((HALO, HALO), 1) <= iota((HALO, HALO), 0)
    for h in range(heads):
        at = head_columns(h)
        top = []
        for m, made in enumerate((queries, keys, values)):
            behind = jnp.where(joined, heard_ends(incoming, m, h, heads), 0.0)
            own = pltpu.roll(tops[m, :, at].astype(f32)[:SHARE], EDGE, 0)
            ext = jnp.where(line < EDGE, behind, own)
            conv = taps[m, 0:1, at] * ext
            for j in range(1, TAPS):
                conv = conv + taps[m, j : j + 1, at] * pltpu.roll(ext, j, 0)
            conv = pltpu.roll(conv, SHARE - EDGE, 0)
            if m < 2:
                sigma = logistic(conv)
                old = (slope_q, slope_k)[m][:SHARE, at]
                top_slope[m, :, at] = jnp.where(line < EDGE, silu_slope(conv, sigma), old)
                conv = conv * sigma
            fresh = to_halo(only_top(conv)).astype(bf16)
            top.append(fresh)
            old = made[:HALO, at]
            top_qkv[m, :, at] = jnp.where(iota((HALO, HEAD_DIM), 0) < EDGE, fresh, old)
        q_top, k_top, v_top = top
        state = jnp.where(joined, state_of(incoming[h * share : (h + 1) * share]), 0.0)
        carried = nn(queries[:, at], (state + tn(k_top, v_top)).astype(bf16))
        attn = local[:, at] + jnp.where(begin <= 0, carried, 0.0)
        scores = jnp.where(causal, nt(q_top, k_top), 0.0).astype(bf16)
        attn_top = nn(scores, v_top) + nn(q_top, state.astype(bf16))
        attn = patched(jnp.where(line < EDGE, attn_top[:SHARE], attn[:SHARE]), attn)
        scale, grad = normed(attn, gain[:, at], cot[:, at].astype(f32))
        out = (attn * scale * gain[:, at]).astype(bf16)
        attn_out[:, :, at] = out.reshape(attn_out.shape[:2] + (HEAD_DIM,))
        grad_norm[:, at] = grad
        q = patched(top_qkv[0, :, at], queries[:, at])
        masked_q = jnp.where(begin < 0, q, jnp.zeros((), bf16))
        back[h * HEAD_DIM : (h + 1) * HEAD_DIM] = tn(masked_q, grad).astype(bf16)


def conv_back(grad, taps, m, starts, first, rows):
    total = grad.shape[0]
    out = taps[m, 0:1] * grad[:rows]
    for j in range(1, TAPS):
        out = out + pltpu.roll(taps[m, j : j + 1] * grad, total - j, 0)[:rows]
    parts = []
    for high in range(CHUNK, rows + 1, CHUNK):
        near = grad[high - SHARE : high + SHARE]
        age = iota((2 * SHARE, HEAD_DIM), 0, high - SHARE)
        age = age - row_starts(starts, first, age)
        end = taps[m, 0:1] * near[:SHARE]
        for j in range(1, TAPS):
            term = jnp.where(age >= j, taps[m, j : j + 1] * near, 0.0)
            end = end + pltpu.roll(term, 2 * SHARE - j, 0)[:SHARE]
        parts.append(out[high - CHUNK : high - SHARE])
        parts.append(end)
    return jnp.concatenate(parts, axis=0).astype(bf16)


def query_kernel(
    starts, keys, values, top_qkv, top_slope, grad_norm, slope, incoming, raw_end, taps, gain,
    attn_out, early, edge_qkv, edge_slope, edge_grad, sem,
):
    rows, width = grad_norm.shape
    heads = width // HEAD_DIM
    share = HEAD_DIM // SHARE
    first = lax.axis_index("seq") * rows
    copy = pltpu.make_async_copy(attn_out, early.at[:, 0], sem)
    copy.start()
    carry = row_starts(starts, first, iota((rows, HEAD_DIM), 0)) < 0
    start = doc_start(starts, first, rows)
    edge_age = iota((2 * HALO, HEAD_DIM), 0, rows - HALO)
    edge_age = edge_age - row_starts(starts, first, edge_age)
    reach = iota((HALO, rows), 1) >= start
    causal = iota((HALO, HALO), 1) <= iota((HALO, HALO), 0)
    for h in range(heads):
        at = head_columns(h)
        state = state_of(incoming[h * share : (h + 1) * share]).astype(bf16)
        k = patched(top_qkv[1, :, at], keys[:, at])
        v = patched(top_qkv[2, :, at], values[:, at])
        g = grad_norm[:, at]
        slope_top = patched(top_slope[0, :, at], slope[:, at])
        edges, slopes = [], []
        for m in range(3):
            after = pltpu.roll(heard_ends(incoming, m, h, heads), SHARE - EDGE, 0)
            after = to_halo(only_top(after))
            ext = jnp.concatenate([raw_end[m, :, at].astype(f32), after], axis=0)
            conv = conv_rows(ext, taps.at[:, :, at], m, edge_age)[HALO:]
            if m < 2:
                sigma = logistic(conv)
                slopes.append(silu_slope(conv, sigma))
                conv = conv * sigma
            edges.append(conv.astype(bf16))
            edge_qkv[m, :, at] = edges[m]
        edge_slope[:, at] = slopes[1]
        q_e, k_e, v_e = edges

        def edge_sums(left, right, right_e, values, values_e, carried):
            scores = jnp.where(reach, nt(left, right), 0.0).astype(bf16)
            scores_e = jnp.where(causal, nt(left, right_e), 0.0).astype(bf16)
            added = jnp.where(start < 0, carried, 0.0)
            return nn(scores, values) + nn(scores_e, values_e) + added

        attn_e = edge_sums(q_e, k, k_e, v, v_e, nn(q_e, state))
        _, g_e = normed(attn_e, gain[:, at], to_halo(next_cot(incoming, h, heads)))
        edge_grad[:, at] = g_e
        grad_q_e = edge_sums(g_e, v, v_e, k, k_e, nt(g_e, state)) * slopes[0]

        parts = []
        for low in range(0, rows, SPAN):
            high = low + SPAN
            scores = behind_mask(nt(g[low:high], v[:high]), low, starts, first)
            parts.append(nn(scores, k[:high]))
        carried = jnp.where(carry, nt(g, state), 0.0)
        grad_q = (jnp.concatenate(parts, axis=0) + carried) * slope_top
        both = jnp.concatenate([grad_q, grad_q_e], axis=0)
        out = conv_back(both, taps.at[:, :, at], 0, starts, first, rows)
        early[:, 1, :, at] = out.reshape((early.shape[0], early.shape[2], HEAD_DIM))
    copy.wait()


def key_kernel(
    starts, queries, keys, values, top_qkv, grad_norm, edge_qkv, edge_grad, local_k, local_v
):
    rows, width = grad_norm.shape
    first = lax.axis_index("seq") * rows
    for h in range(width // HEAD_DIM):
        at = head_columns(h)
        columns = (queries[:, at], keys[:, at], values[:, at])
        q, k, v = [patched(top_qkv[m, :, at], columns[m]) for m in range(3)]
        g = grad_norm[:, at]
        for low in range(0, rows, SPAN):
            high = low + SPAN
            scores = ahead_mask(nt(v[low:high], g[low:]), low, starts, first)
            local_k[low:high, at] = nn(scores, q[low:]).astype(bf16)
            scores = ahead_mask(nt(k[low:high], q[low:]), low, starts, first)
            local_v[low:high, at] = nn(scores, g[low:]).astype(bf16)
        q_e, k_e, v_e = edge_qkv[0, :, at], edge_qkv[1, :, at], edge_qkv[2, :, at]
        g_e = edge_grad[:, at]
        earlier = iota((HALO, HALO), 1) < iota((HALO, HALO), 0)
        scores = jnp.where(earlier, -nt(v_e, g_e), 0.0).astype(bf16)
        local_k[rows:, at] = nn(scores, q_e).astype(bf16)
        scores = jnp.where(earlier, -nt(k_e, q_e), 0.0).astype(bf16)
        local_v[rows:, at] = nn(scores, g_e).astype(bf16)


def last_kernel(
    starts, keys, values, top_qkv, top_slope, edge_qkv, slope, edge_slope, local_k, local_v,
    future, taps, early, sent, sem,
):
    total, width = local_k.shape
    rows = total - HALO
    first = lax.axis_index("seq") * rows
    copy = pltpu.make_async_copy(early, sent.at[:, pl.ds(0, 2)], sem)
    copy.start()
    after = iota((total, HEAD_DIM), 0) >= doc_start(starts, first, rows)
    shape = (sent.shape[0], sent.shape[2], HEAD_DIM)
    for m in (2, 1):
        for h in range(width // HEAD_DIM):
            at = head_columns(h)
            state = future[h * HEAD_DIM : (h + 1) * HEAD_DIM]
            if m == 2:
                k = patched(top_qkv[1, :, at], keys[:, at])
                k = jnp.concatenate([k, edge_qkv[1, :, at]], axis=0)
                grad = local_v[:, at].astype(f32) + jnp.where(after, nn(k, state), 0.0)
            else:
                v = patched(top_qkv[2, :, at], values[:, at])
                v = jnp.concatenate([v, edge_qkv[2, :, at]], axis=0)
                slopes = patched(top_slope[1, :, at], slope[:, at])
                slopes = jnp.concatenate([slopes, edge_slope[:, at]], axis=0)
                grad = (local_k[:, at].astype(f32) + jnp.where(after, nt(v, state), 0.0)) * slopes
            out = conv_back(grad, taps.at[:, :, at], m, starts, first, rows)
            sent[:, m + 1, :, at] = out.reshape(shape)
    copy.wait()


def closed(starts, rows, i):
    found = jnp.bool_(False)
    for d in range(starts.shape[0]):
        found = found | ((starts[d] >= i * rows) & (starts[d] < (i + 1) * rows))
    return found


def forward_kernel(rows, starts, sums, taps, out):
    count = sums.shape[0]
    share = HEAD_DIM // SHARE
    place = lax.axis_index("seq")
    part, head = lax.rem(place, share), lax.div(place, share)
    line = iota((SHARE, HEAD_DIM), 0)
    inside = (line >= EDGE) & (line < 2 * EDGE)
    nothing = jnp.zeros((SHARE, HEAD_DIM), f32)

    def tap(m, j):
        row = taps[m, j : j + 1, :HEAD_DIM]
        for h in range(1, taps.shape[2] // HEAD_DIM):
            row = jnp.where(head == h, taps[m, j : j + 1, head_columns(h)], row)
        return row

    heard = [sums[i].astype(f32) for i in range(count)]
    ends = {m: [block[m * SHARE : (m + 1) * SHARE] for block in heard] for m in (1, 2)}
    tops = {1: [], 2: []}
    for m in (1, 2):
        weights = [tap(m, j) for j in range(TAPS)]
        for i in range(count):
            begun, split = jnp.bool_(False), jnp.bool_(False)
            for d in range(starts.shape[0]):
                begun = begun | (starts[d] == i * rows)
                split = split | ((starts[d] > i * rows) & (starts[d] < (i + 1) * rows))
            behind = jnp.where(begun, 0.0, ends[m][i - 1]) if i else nothing
            ext = jnp.where(line < EDGE, behind, ends[m][i])
            conv = weights[0] * ext
            for j in range(1, TAPS):
                conv = conv + weights[j] * pltpu.roll(ext, j, 0)
            if m == 1:
                conv = jnp.where(split, 0.0, conv * logistic(conv))
            tops[m].append(jnp.where(inside, conv, 0.0))
    k_tops, v_tops = [jnp.concatenate(tops[m], axis=0).astype(bf16) for m in (1, 2)]
    own = iota((SHARE, HEAD_DIM), 1) == line + part * SHARE
    picked = nt(jnp.where(own, 1.0, 0.0).astype(bf16), k_tops)
    size = count * SHARE
    same = lax.div(iota((size, size), 0), SHARE) == lax.div(iota((size, size), 1), SHARE)
    picked = jnp.where(same, jnp.concatenate([picked] * count, axis=0), 0.0).astype(bf16)
    added = nn(picked, v_tops)
    state = nothing
    for i in range(count):
        sides = []
        for j in (i - 1, i + 1):
            if 0 <= j < count:
                sides.append((jnp.where(lax.rem(part, 2) == 0, ends[1][j], ends[2][j]), ends[1][j]))
            else:
                sides.append((nothing, nothing))
        block = jnp.where(line < EDGE, sides[0][0], sides[1][0])
        route = jnp.where(place < EDGE * (taps.shape[2] // HEAD_DIM), sides[0][1], sides[1][1])
        block = jnp.where(line == ROUTE, route, block)
        out[i] = jnp.concatenate([state, block], axis=0).astype(bf16)
        new = heard[i][:SHARE] + added[i * SHARE : (i + 1) * SHARE]
        state = new + jnp.where(closed(starts, rows, i), 0.0, state)


def backward_kernel(rows, starts, sums, out):
    count = 2 * sums.shape[0]
    state = jnp.zeros((SHARE, HEAD_DIM), f32)
    for i in range(count - 1, 0, -2):
        pair = sums[i // 2].astype(f32)
        upper = state
        state = pair[SHARE:] + jnp.where(closed(starts, rows, i), 0.0, state)
        out[i // 2] = jnp.concatenate([state, upper], axis=0).astype(bf16)
        state = pair[:SHARE] + jnp.where(closed(starts, rows, i - 1), 0.0, state)


def gather_kernel(sent, out, grad):
    count, _, _, width = sent.shape
    for i in range(count):
        columns = slice(i * width, (i + 1) * width)
        out[:, columns] = sent[i, 0]
        for m in range(3):
            grad[m, :, columns] = sent[i, m + 1]


def shards(qkv_raw, conv_weight, norm_gain, doc_starts, cotangent):
    rows = qkv_raw.shape[0]
    width = qkv_raw.shape[2]
    heads = width // HEAD_DIM
    total = rows + HALO
    devices = lax.axis_size("seq")
    columns = lax.axis_size("head")
    piece = rows // columns
    share = devices // heads
    raw = qkv_raw.transpose(1, 0, 2)
    in_hbm = functools.partial(pltpu.with_memory_space_constraint, memory_space=pltpu.HBM)
    hd = HEAD_DIM


    smem = pl.BlockSpec(memory_space=pltpu.SMEM)
    params = pltpu.CompilerParams(vmem_limit_bytes=16 * 1024 * 1024)

    vmem = pl.BlockSpec(memory_space=pltpu.VMEM)
    hbm = pl.BlockSpec(memory_space=pltpu.HBM)
    dma = pltpu.SemaphoreType.DMA

    def flat_call(body, ins, outs, scratch, *args):
        spec = hbm if body is conv_kernel else smem
        return pl.pallas_call(
            body,
            in_specs=[spec] + ins,
            out_specs=[hbm if out.memory_space == pltpu.HBM else vmem for out in outs],
            out_shape=outs,
            scratch_shapes=scratch,
            compiler_params=params,
        )(in_hbm(doc_starts) if spec is hbm else doc_starts, *[in_hbm(a) if spec is hbm else a for a, spec in zip(args, ins)])

    wide = pltpu.VMEM((rows, width), bf16)
    tall = pltpu.VMEM((rows, width), f32)
    keys, values, message, raw_end, tops, taps, gain = flat_call(
        conv_kernel,
        [hbm] * 4,
        [
            wide, wide, pltpu.VMEM((devices, 3 * SHARE, hd), bf16),
            pltpu.VMEM((3, HALO, width), bf16), pltpu.VMEM((4, HALO, width), bf16),
            pltpu.VMEM(conv_weight.shape, f32), pltpu.VMEM((1, width), f32),
        ],
        [pltpu.VMEM((2, rows, width), bf16), pltpu.SMEM(doc_starts.shape, jnp.int32), dma((8,))],
        raw, cotangent, conv_weight, norm_gain.reshape(1, width),
    )

    def swap(parts):
        return lax.all_to_all(parts, "seq", 0, 0, tiled=True)

    def scan(body, shape, parts, *others):
        (found,) = flat_call(
            functools.partial(body, rows), [vmem] * (1 + len(others)),
            [pltpu.VMEM(shape, bf16)], [], parts, *others,
        )
        return found

    beside = flat_call(
        local_kernel, [hbm] + [vmem] * 3, [wide, tall, tall, tall],
        [pltpu.VMEM((2, rows, width), bf16), dma((2,))],
        raw, taps, keys, values,
    )
    message, beside = lax.optimization_barrier((swap(message), beside))
    queries, slope_q, slope_k, local = beside
    message = scan(forward_kernel, (devices, 2 * SHARE, hd), message, taps)
    incoming = swap(message)
    attn_out, grad_norm, back, top_qkv, top_slope = flat_call(
        norm_kernel,
        [vmem] * 11,
        [
            pltpu.VMEM((columns, piece, width), bf16), wide,
            pltpu.VMEM((heads * hd, hd), bf16), pltpu.VMEM((3, HALO, width), bf16),
            pltpu.VMEM((2, SHARE, width), f32),
        ],
        [],
        queries, local, incoming, cotangent, gain, tops, taps, slope_q, slope_k, keys, values,
    )
    early, edge_qkv, edge_slope, edge_grad = flat_call(
        query_kernel,
        [vmem] * 11,
        [
            pltpu.VMEM((columns, 2, piece, width), bf16), pltpu.VMEM((3, HALO, width), bf16),
            pltpu.VMEM((HALO, width), f32), pltpu.VMEM((HALO, width), bf16),
        ],
        [dma(())],
        keys, values, top_qkv, top_slope, grad_norm, slope_q, incoming, raw_end, taps, gain,
        attn_out,
    )
    back = swap(back.reshape(devices, SHARE, hd))
    back, early, edge_qkv, edge_slope, edge_grad = lax.optimization_barrier(
        (back, early, edge_qkv, edge_slope, edge_grad)
    )
    pairs = (devices // 2, 2 * SHARE, hd)
    back = scan(backward_kernel, pairs, back.reshape(pairs))
    local_k, local_v = flat_call(
        key_kernel, [vmem] * 7, [pltpu.VMEM((total, width), bf16)] * 2, [],
        queries, keys, values, top_qkv, grad_norm, edge_qkv, edge_grad,
    )
    future, local_k, local_v = lax.optimization_barrier((swap(back.reshape(devices, SHARE, hd)), local_k, local_v))
    (sent,) = flat_call(
        last_kernel, [vmem] * 12, [pltpu.VMEM((columns, 4, piece, width), bf16)], [dma(())],
        keys, values, top_qkv, top_slope, edge_qkv, slope_k, edge_slope, local_k, local_v,
        future.reshape(heads * hd, hd), taps, early,
    )
    sent = lax.all_to_all(sent, "head", 0, 0, tiled=True)
    out, grad = pl.pallas_call(
        gather_kernel,
        out_shape=[
            jax.ShapeDtypeStruct((piece, columns * width), bf16),
            jax.ShapeDtypeStruct((3, piece, columns * width), bf16),
        ],
        compiler_params=params,
    )(sent)
    return out, grad.transpose(1, 0, 2)


def solution(mesh):
    return jax.shard_map(
        shards,
        mesh=mesh,
        in_specs=(P("seq", None, "head"), P(None, None, "head"), P("head"), P(), P("seq", "head")),
        out_specs=(P(("seq", "head"), None), P(("seq", "head"), None, None)),
        check_vma=False,
    )
```

```python
import functools

import jax
import jax.numpy as jnp
from jax import lax
from jax.experimental import pallas as pl
from jax.experimental.pallas import tpu as pltpu
from jax.sharding import PartitionSpec as P

HEAD_DIM = 128
TAPS = 4
CHUNK = 128
SPAN = 256
HALO = 16
EDGE = TAPS - 1
ROUTE = 2 * EDGE
SHARE = 8
FAR = 1 << 30

f32 = jnp.float32
bf16 = jnp.bfloat16


def nt(a, b):
    return lax.dot_general(a, b, (((1,), (1,)), ((), ())), preferred_element_type=f32)


def nn(a, b):
    return lax.dot_general(a, b, (((1,), (0,)), ((), ())), preferred_element_type=f32)


def tn(a, b):
    return lax.dot_general(a, b, (((0,), (0,)), ((), ())), preferred_element_type=f32)


def doc_start(starts, first, pos):
    found = jnp.int32(-FAR)
    for d in range(starts.shape[0]):
        rel = starts[d] - first
        found = jnp.maximum(found, jnp.where(rel <= pos, rel, -FAR))
    return found


def doc_end(starts, first, pos):
    found = jnp.int32(FAR)
    for d in range(starts.shape[0]):
        rel = starts[d] - first
        found = jnp.minimum(found, jnp.where(rel > pos, rel, FAR))
    return found


def row_starts(starts, first, rows):
    found = jnp.full(rows.shape, -FAR, jnp.int32)
    for d in range(starts.shape[0]):
        rel = starts[d] - first
        found = jnp.maximum(found, jnp.where(rows >= rel, rel, -FAR))
    return found


def iota(shape, axis, base=0):
    return lax.broadcasted_iota(jnp.int32, shape, axis) + base


def conv_rows(ext, taps, m, age):
    conv = taps[m, 0:1] * ext
    for j in range(1, TAPS):
        conv = conv + jnp.where(age >= j, taps[m, j : j + 1] * pltpu.roll(ext, j, 0), 0.0)
    return conv


def logistic(x):
    return 1.0 / (1.0 + jnp.exp(-x))


def silu_slope(conv, sigma):
    return sigma * (1.0 + conv * (1.0 - sigma))


def conv_docs(ext, taps, m, starts, first):
    rows = ext.shape[0] - HALO
    conv = taps[m, 0:1] * ext
    for j in range(1, TAPS):
        conv = conv + taps[m, j : j + 1] * pltpu.roll(ext, j, 0)
    parts = []
    for low in range(0, rows, CHUNK):
        top = ext[HALO + low - SHARE : HALO + low + SHARE]
        age = iota((2 * SHARE, HEAD_DIM), 0, low - SHARE) - doc_start(starts, first, low)
        parts.append(conv_rows(top, taps, m, age)[SHARE:])
        parts.append(conv[HALO + low + SHARE : HALO + low + CHUNK])
    return jnp.concatenate(parts, axis=0)


def behind_mask(scores, low, starts, first, least=0):
    size, high = scores.shape
    causal = iota((CHUNK, CHUNK), 1) <= iota((CHUNK, CHUNK), 0)
    late = iota((CHUNK, CHUNK), 1) >= least
    bands = []
    for top in range(low, low + size, CHUNK):
        begin = doc_start(starts, first, top)
        parts = []
        for at in range(0, high, CHUNK):
            part = scores[top - low : top - low + CHUNK, at : at + CHUNK]
            if at > top:
                part = jnp.zeros_like(part)
            elif at == top:
                part = jnp.where(causal & late if at == 0 and least else causal, part, 0.0)
            else:
                part = jnp.where(at >= begin, part, 0.0)
                if at == 0 and least:
                    part = jnp.where(late, part, 0.0)
            parts.append(part)
        bands.append(jnp.concatenate(parts, axis=1))
    return jnp.concatenate(bands, axis=0).astype(bf16)


def ahead_mask(scores, low, starts, first):
    size, length = scores.shape
    causal = iota((CHUNK, CHUNK), 1) >= iota((CHUNK, CHUNK), 0)
    bands = []
    for top in range(low, low + size, CHUNK):
        end = doc_end(starts, first, top)
        parts = []
        for at in range(low, low + length, CHUNK):
            part = scores[top - low : top - low + CHUNK, at - low : at - low + CHUNK]
            if at < top:
                part = jnp.zeros_like(part)
            elif at == top:
                part = jnp.where(causal, part, 0.0)
            else:
                part = jnp.where(at < end, part, 0.0)
            parts.append(part)
        bands.append(jnp.concatenate(parts, axis=1))
    return jnp.concatenate(bands, axis=0).astype(bf16)


def head_columns(h):
    return slice(h * HEAD_DIM, (h + 1) * HEAD_DIM)


def spread(row):
    return jnp.broadcast_to(row, (SHARE, HEAD_DIM))


def only_top(block):
    return jnp.where(iota(block.shape, 0) < EDGE, block, jnp.zeros((), block.dtype))


def conv_kernel(
    starts_far, raw_far, cot_far, taps_far, gain_far,
    keys, values, message, rims, taps, raw, gain, starts, sems,
):
    _, rows, width = raw.shape
    heads = range(width // HEAD_DIM)
    first = lax.axis_index("seq") * rows
    taps_load = pltpu.make_async_copy(taps_far, taps.at[pl.ds(0, 3)], sems.at[0])
    loads = [pltpu.make_async_copy(raw_far.at[m], raw.at[m - 1], sems.at[m]) for m in (1, 2)]
    others = [
        pltpu.make_async_copy(raw_far.at[:, pl.ds(0, HALO)], rims.at[pl.ds(0, 3)], sems.at[3]),
        pltpu.make_async_copy(cot_far.at[pl.ds(0, HALO)], rims.at[3], sems.at[4]),
        pltpu.make_async_copy(
            raw_far.at[:, pl.ds(rows - HALO, HALO)], rims.at[pl.ds(4, 3)], sems.at[5]
        ),
        pltpu.make_async_copy(gain_far, gain, sems.at[6]),
    ]
    starts_load = pltpu.make_async_copy(starts_far, starts, sems.at[7])
    for load in [starts_load, loads[0], taps_load, loads[1]] + others:
        load.start()
    starts_load.wait()
    taps_load.wait()
    begin = jnp.maximum(doc_start(starts, first, rows - 1), EDGE)
    keep = iota((rows, HEAD_DIM), 0) >= begin
    made = {}
    for m, out in ((1, keys), (2, values)):
        loads[m - 1].wait()
        for h in heads:
            at = head_columns(h)
            ext = jnp.concatenate(
                [jnp.zeros((HALO, HEAD_DIM), f32), raw[m - 1, :, at].astype(f32)], axis=0
            )
            conv = conv_docs(ext, taps.at[:, :, at], m, starts, first)
            if m == 1:
                conv = conv * logistic(conv)
            made[m, h] = conv.astype(bf16)
            out[:, at] = made[m, h]
    for load in others:
        load.wait()
    taps[3] = jnp.broadcast_to(gain[...], (TAPS, width))
    share = HEAD_DIM // SHARE
    line = iota((SHARE, HEAD_DIM), 0)
    ends, routed = {}, []
    for h in heads:
        at = head_columns(h)
        for m in range(3):
            low = rims[4 + m, :, at].astype(f32)[HALO - SHARE :]
            top = rims[m, :, at].astype(f32)[:SHARE]
            ends[m, h] = pltpu.roll(jnp.where(line >= SHARE - EDGE, low, top), EDGE, 0)
    for base in (0, EDGE):
        for h in heads:
            routed += [ends[0, h][base + a : base + a + 1] for a in range(EDGE)]
    for h in heads:
        top = rims[3, :, head_columns(h)].astype(f32)
        routed += [top[a : a + 1] for a in range(EDGE)]
    parts = []
    for h in heads:
        summary = tn(jnp.where(keep, made[1, h], jnp.zeros((), bf16)), made[2, h])
        for n in range(share):
            r = h * share + n
            k_ends = ends[1, h]
            if r < len(routed):
                k_ends = jnp.where(line == ROUTE, spread(routed[r]), k_ends)
            parts += [summary[n * SHARE : (n + 1) * SHARE], k_ends, ends[2, h]]
            if r % 2:
                message[r // 2] = jnp.concatenate(parts, axis=0).astype(bf16)
                parts = []


def local_kernel(
    starts, raw_far, taps, keys, values, queries, slope_q, slope_k, local, raw, sems
):
    rows, width = local.shape
    first = lax.axis_index("seq") * rows
    loads = [pltpu.make_async_copy(raw_far.at[m], raw.at[m], sems.at[m]) for m in range(2)]
    for load in loads:
        load.start()
    for m, slope in ((0, slope_q), (1, slope_k)):
        loads[m].wait()
        for h in range(width // HEAD_DIM):
            at = head_columns(h)
            ext = jnp.concatenate(
                [jnp.zeros((HALO, HEAD_DIM), f32), raw[m, :, at].astype(f32)], axis=0
            )
            conv = conv_docs(ext, taps.at[:, :, at], m, starts, first)
            sigma = logistic(conv)
            slope[:, at] = silu_slope(conv, sigma).astype(bf16)
            if m == 0:
                queries[:, at] = (conv * sigma).astype(bf16)
    for h in range(width // HEAD_DIM):
        at = head_columns(h)
        for low in range(0, rows, SPAN):
            high = low + SPAN
            scores = nt(queries[low:high, at], keys[:high, at])
            scores = behind_mask(scores, low, starts, first, EDGE)
            local[low:high, at] = nn(scores, values[:high, at])


def state_of(message):
    return message.astype(f32)[:, :SHARE].reshape(HEAD_DIM, HEAD_DIM)


def heard_ends(incoming, m, h, heads):
    share = HEAD_DIM // SHARE
    if m:
        return incoming[h * share + m - 1].astype(f32)[SHARE:]
    line = iota((SHARE, HEAD_DIM), 0)
    block = jnp.zeros((SHARE, HEAD_DIM), f32)
    for a in range(2 * EDGE):
        r = (a // EDGE * heads + h) * EDGE + a % EDGE
        row = incoming[r].astype(f32)[SHARE + ROUTE : SHARE + ROUTE + 1]
        block = jnp.where(line == a, spread(row), block)
    return block


def next_cot(incoming, h, heads):
    line = iota((SHARE, HEAD_DIM), 0)
    block = jnp.zeros((SHARE, HEAD_DIM), f32)
    for a in range(EDGE):
        r = (2 * heads + h) * EDGE + a
        row = incoming[r].astype(f32)[SHARE + ROUTE : SHARE + ROUTE + 1]
        block = jnp.where(line == a, spread(row), block)
    return block


def to_halo(block):
    return jnp.concatenate([block, jnp.zeros((HALO - SHARE, HEAD_DIM), block.dtype)], axis=0)


def patched(top, column):
    return jnp.concatenate([top, column[top.shape[0] :]], axis=0)


def normed(attn, gains, cots):
    msq = jnp.mean(attn * attn, axis=-1, keepdims=True)
    scale = lax.rsqrt(jnp.maximum(msq, 1.0))
    scaled = cots * gains
    inner = jnp.mean(scaled * attn, axis=-1, keepdims=True)
    factor = jnp.where(msq > 1.0, scale * scale * scale * inner, 0.0)
    return scale, (scale * scaled - attn * factor).astype(bf16)


def norm_kernel(
    starts, queries, local, incoming, cot, rims, taps, slope_q, slope_k, keys, values,
    attn_out, grad_norm, back, top_qkv, top_slope,
):
    rows, width = local.shape
    heads = width // HEAD_DIM
    share = HEAD_DIM // SHARE
    gain = taps.at[3, pl.ds(0, 1)]
    first = lax.axis_index("seq") * rows
    begin = row_starts(starts, first, iota((rows, HEAD_DIM), 0))
    joined = doc_start(starts, first, 0) < 0
    line = iota((SHARE, HEAD_DIM), 0)
    causal = iota((HALO, HALO), 1) <= iota((HALO, HALO), 0)
    for h in range(heads):
        at = head_columns(h)
        top = []
        for m, made in enumerate((queries, keys, values)):
            behind = jnp.where(joined, heard_ends(incoming, m, h, heads), 0.0)
            own = pltpu.roll(rims[m, :, at].astype(f32)[:SHARE], EDGE, 0)
            ext = jnp.where(line < EDGE, behind, own)
            conv = taps[m, 0:1, at] * ext
            for j in range(1, TAPS):
                conv = conv + taps[m, j : j + 1, at] * pltpu.roll(ext, j, 0)
            conv = pltpu.roll(conv, SHARE - EDGE, 0)
            if m < 2:
                sigma = logistic(conv)
                old = (slope_q, slope_k)[m][:HALO, at].astype(f32)[:SHARE]
                top_slope[m, :, at] = jnp.where(line < EDGE, silu_slope(conv, sigma), old)
                conv = conv * sigma
            fresh = to_halo(only_top(conv)).astype(bf16)
            top.append(fresh)
            old = made[:HALO, at]
            top_qkv[m, :, at] = jnp.where(iota((HALO, HEAD_DIM), 0) < EDGE, fresh, old)
        q_top, k_top, v_top = top
        state = jnp.where(joined, state_of(incoming[h * share : (h + 1) * share]), 0.0)
        carried = nn(queries[:, at], (state + tn(k_top, v_top)).astype(bf16))
        attn = local[:, at] + jnp.where(begin <= 0, carried, 0.0)
        scores = jnp.where(causal, nt(q_top, k_top), 0.0).astype(bf16)
        attn_top = nn(scores, v_top) + nn(q_top, state.astype(bf16))
        attn = patched(jnp.where(line < EDGE, attn_top[:SHARE], attn[:SHARE]), attn)
        scale, grad = normed(attn, gain[:, at], cot[:, at].astype(f32))
        out = (attn * scale * gain[:, at]).astype(bf16)
        attn_out[:, :, at] = out.reshape(attn_out.shape[:2] + (HEAD_DIM,))
        grad_norm[:, at] = grad
        q = patched(top_qkv[0, :, at], queries[:, at])
        masked_q = jnp.where(begin < 0, q, jnp.zeros((), bf16))
        back[h * HEAD_DIM : (h + 1) * HEAD_DIM] = tn(masked_q, grad).astype(bf16)


def conv_back(grad, taps, m, starts, first, rows):
    total = grad.shape[0]
    out = taps[m, 0:1] * grad[:rows]
    for j in range(1, TAPS):
        out = out + pltpu.roll(taps[m, j : j + 1] * grad, total - j, 0)[:rows]
    parts = []
    for high in range(CHUNK, rows + 1, CHUNK):
        near = grad[high - SHARE : high + SHARE]
        age = iota((2 * SHARE, HEAD_DIM), 0, high - SHARE)
        age = age - row_starts(starts, first, age)
        end = taps[m, 0:1] * near[:SHARE]
        for j in range(1, TAPS):
            term = jnp.where(age >= j, taps[m, j : j + 1] * near, 0.0)
            end = end + pltpu.roll(term, 2 * SHARE - j, 0)[:SHARE]
        parts.append(out[high - CHUNK : high - SHARE])
        parts.append(end)
    return jnp.concatenate(parts, axis=0).astype(bf16)


def query_kernel(
    starts, keys, values, top_qkv, top_slope, grad_norm, slope, incoming, rims, taps,
    out_q, edge_qkv, edge_slope, edge_grad,
):
    rows, width = grad_norm.shape
    heads = width // HEAD_DIM
    share = HEAD_DIM // SHARE
    first = lax.axis_index("seq") * rows
    carry = row_starts(starts, first, iota((rows, HEAD_DIM), 0)) < 0
    start = doc_start(starts, first, rows)
    edge_age = iota((2 * HALO, HEAD_DIM), 0, rows - HALO)
    edge_age = edge_age - row_starts(starts, first, edge_age)
    reach = iota((HALO, rows), 1) >= start
    causal = iota((HALO, HALO), 1) <= iota((HALO, HALO), 0)
    for h in range(heads):
        at = head_columns(h)
        state = state_of(incoming[h * share : (h + 1) * share]).astype(bf16)
        k = patched(top_qkv[1, :, at], keys[:, at])
        v = patched(top_qkv[2, :, at], values[:, at])
        g = grad_norm[:, at]
        slope_top = patched(top_slope[0, :, at], slope[:, at].astype(f32))
        edges, slopes = [], []
        for m in range(3):
            after = pltpu.roll(heard_ends(incoming, m, h, heads), SHARE - EDGE, 0)
            after = to_halo(only_top(after))
            ext = jnp.concatenate([rims[4 + m, :, at].astype(f32), after], axis=0)
            conv = conv_rows(ext, taps.at[:, :, at], m, edge_age)[HALO:]
            if m < 2:
                sigma = logistic(conv)
                slopes.append(silu_slope(conv, sigma))
                conv = conv * sigma
            edges.append(conv.astype(bf16))
            edge_qkv[m, :, at] = edges[m]
        edge_slope[:, at] = slopes[1]
        q_e, k_e, v_e = edges

        def edge_sums(left, right, right_e, values, values_e, carried):
            scores = jnp.where(reach, nt(left, right), 0.0).astype(bf16)
            scores_e = jnp.where(causal, nt(left, right_e), 0.0).astype(bf16)
            added = jnp.where(start < 0, carried, 0.0)
            return nn(scores, values) + nn(scores_e, values_e) + added

        attn_e = edge_sums(q_e, k, k_e, v, v_e, nn(q_e, state))
        _, g_e = normed(attn_e, taps[3, 0:1, at], to_halo(next_cot(incoming, h, heads)))
        edge_grad[:, at] = g_e
        grad_q_e = edge_sums(g_e, v, v_e, k, k_e, nt(g_e, state)) * slopes[0]

        parts = []
        for low in range(0, rows, SPAN):
            high = low + SPAN
            scores = behind_mask(nt(g[low:high], v[:high]), low, starts, first)
            parts.append(nn(scores, k[:high]))
        carried = jnp.where(carry, nt(g, state), 0.0)
        grad_q = (jnp.concatenate(parts, axis=0) + carried) * slope_top
        both = jnp.concatenate([grad_q, grad_q_e], axis=0)
        out = conv_back(both, taps.at[:, :, at], 0, starts, first, rows)
        out_q[:, :, at] = out.reshape(out_q.shape[:2] + (HEAD_DIM,))


def key_kernel(
    starts, queries, keys, values, top_qkv, grad_norm, edge_qkv, edge_grad, local_k, local_v
):
    rows, width = grad_norm.shape
    first = lax.axis_index("seq") * rows
    for h in range(width // HEAD_DIM):
        at = head_columns(h)
        columns = (queries[:, at], keys[:, at], values[:, at])
        q, k, v = [patched(top_qkv[m, :, at], columns[m]) for m in range(3)]
        g = grad_norm[:, at]
        for low in range(0, rows, SPAN):
            high = low + SPAN
            scores = ahead_mask(nt(v[low:high], g[low:]), low, starts, first)
            local_k[low:high, at] = nn(scores, q[low:]).astype(bf16)
            scores = ahead_mask(nt(k[low:high], q[low:]), low, starts, first)
            local_v[low:high, at] = nn(scores, g[low:]).astype(bf16)
        q_e, k_e, v_e = edge_qkv[0, :, at], edge_qkv[1, :, at], edge_qkv[2, :, at]
        g_e = edge_grad[:, at]
        earlier = iota((HALO, HALO), 1) < iota((HALO, HALO), 0)
        scores = jnp.where(earlier, -nt(v_e, g_e), 0.0).astype(bf16)
        local_k[rows:, at] = nn(scores, q_e).astype(bf16)
        scores = jnp.where(earlier, -nt(k_e, q_e), 0.0).astype(bf16)
        local_v[rows:, at] = nn(scores, g_e).astype(bf16)


def gradient_kernel(
    starts, queries, keys, values, top_qkv, top_slope, grad_norm, slope, incoming, rims, taps,
    out_q, edge_qkv, edge_slope, local_k, local_v, edge_grad,
):
    query_kernel(
        starts, keys, values, top_qkv, top_slope, grad_norm, slope, incoming, rims, taps,
        out_q, edge_qkv, edge_slope, edge_grad,
    )
    key_kernel(
        starts, queries, keys, values, top_qkv, grad_norm, edge_qkv, edge_grad, local_k, local_v
    )


def last_kernel(
    starts, keys, values, top_qkv, top_slope, edge_qkv, slope, edge_slope, local_k, local_v,
    future, taps, attn_out, out_q, sent, sems,
):
    total, width = local_k.shape
    rows = total - HALO
    first = lax.axis_index("seq") * rows
    copies = [
        pltpu.make_async_copy(part, sent.at[:, n], sems.at[n])
        for n, part in enumerate((attn_out, out_q))
    ]
    for copy in copies:
        copy.start()
    after = iota((total, HEAD_DIM), 0) >= doc_start(starts, first, rows)
    shape = (sent.shape[0], sent.shape[2], HEAD_DIM)
    for m in (2, 1):
        for h in range(width // HEAD_DIM):
            at = head_columns(h)
            state = future[h * HEAD_DIM : (h + 1) * HEAD_DIM]
            if m == 2:
                k = patched(top_qkv[1, :, at], keys[:, at])
                k = jnp.concatenate([k, edge_qkv[1, :, at]], axis=0)
                grad = local_v[:, at].astype(f32) + jnp.where(after, nn(k, state), 0.0)
            else:
                v = patched(top_qkv[2, :, at], values[:, at])
                v = jnp.concatenate([v, edge_qkv[2, :, at]], axis=0)
                slopes = patched(top_slope[1, :, at], slope[:, at].astype(f32))
                slopes = jnp.concatenate([slopes, edge_slope[:, at]], axis=0)
                grad = (local_k[:, at].astype(f32) + jnp.where(after, nt(v, state), 0.0)) * slopes
            out = conv_back(grad, taps.at[:, :, at], m, starts, first, rows)
            sent[:, m + 1, :, at] = out.reshape(shape)
    for copy in copies:
        copy.wait()


def closed(starts, rows, i):
    found = jnp.bool_(False)
    for d in range(starts.shape[0]):
        found = found | ((starts[d] >= i * rows) & (starts[d] < (i + 1) * rows))
    return found


def forward_kernel(rows, starts, sums, taps, out):
    count = 2 * sums.shape[0]
    share = HEAD_DIM // SHARE
    place = lax.axis_index("seq")
    part, head = lax.rem(place, share), lax.div(place, share)
    line = iota((SHARE, HEAD_DIM), 0)
    inside = (line >= EDGE) & (line < 2 * EDGE)
    nothing = jnp.zeros((SHARE, HEAD_DIM), f32)

    def tap(m, j):
        row = taps[m, j : j + 1, :HEAD_DIM]
        for h in range(1, taps.shape[2] // HEAD_DIM):
            row = jnp.where(head == h, taps[m, j : j + 1, head_columns(h)], row)
        return row

    heard = []
    for i in range(count // 2):
        pair = sums[i].astype(f32)
        heard += [pair[: 3 * SHARE], pair[3 * SHARE :]]
    ends = {m: [block[m * SHARE : (m + 1) * SHARE] for block in heard] for m in (1, 2)}
    tops = {1: [], 2: []}
    for m in (1, 2):
        weights = [tap(m, j) for j in range(TAPS)]
        for i in range(count):
            begun, split = jnp.bool_(False), jnp.bool_(False)
            for d in range(starts.shape[0]):
                begun = begun | (starts[d] == i * rows)
                split = split | ((starts[d] > i * rows) & (starts[d] < (i + 1) * rows))
            behind = jnp.where(begun, 0.0, ends[m][i - 1]) if i else nothing
            ext = jnp.where(line < EDGE, behind, ends[m][i])
            conv = weights[0] * ext
            for j in range(1, TAPS):
                conv = conv + weights[j] * pltpu.roll(ext, j, 0)
            if m == 1:
                conv = jnp.where(split, 0.0, conv * logistic(conv))
            tops[m].append(jnp.where(inside, conv, 0.0))
    k_tops, v_tops = [jnp.concatenate(tops[m], axis=0).astype(bf16) for m in (1, 2)]
    own = iota((SHARE, HEAD_DIM), 1) == line + part * SHARE
    picked = nt(jnp.where(own, 1.0, 0.0).astype(bf16), k_tops)
    size = count * SHARE
    same = lax.div(iota((size, size), 0), SHARE) == lax.div(iota((size, size), 1), SHARE)
    picked = jnp.where(same, jnp.concatenate([picked] * count, axis=0), 0.0).astype(bf16)
    added = nn(picked, v_tops)
    state = nothing
    for i in range(count):
        sides = []
        for j in (i - 1, i + 1):
            if 0 <= j < count:
                sides.append((jnp.where(lax.rem(part, 2) == 0, ends[1][j], ends[2][j]), ends[1][j]))
            else:
                sides.append((nothing, nothing))
        block = jnp.where(line < EDGE, sides[0][0], sides[1][0])
        route = jnp.where(place < EDGE * (taps.shape[2] // HEAD_DIM), sides[0][1], sides[1][1])
        block = jnp.where(line == ROUTE, route, block)
        out[i] = jnp.concatenate([state, block], axis=0).astype(bf16)
        new = heard[i][:SHARE] + added[i * SHARE : (i + 1) * SHARE]
        state = new + jnp.where(closed(starts, rows, i), 0.0, state)


def backward_kernel(rows, starts, sums, out):
    count = 2 * sums.shape[0]
    state = jnp.zeros((SHARE, HEAD_DIM), f32)
    for i in range(count - 1, 0, -2):
        pair = sums[i // 2].astype(f32)
        upper = state
        state = pair[SHARE:] + jnp.where(closed(starts, rows, i), 0.0, state)
        out[i // 2] = jnp.concatenate([state, upper], axis=0).astype(bf16)
        state = pair[:SHARE] + jnp.where(closed(starts, rows, i - 1), 0.0, state)


def gather_kernel(sent, out, grad):
    count, _, _, width = sent.shape
    for i in range(count):
        columns = slice(i * width, (i + 1) * width)
        out[:, columns] = sent[i, 0]
        for m in range(3):
            grad[m, :, columns] = sent[i, m + 1]


def shards(qkv_raw, conv_weight, norm_gain, doc_starts, cotangent):
    rows = qkv_raw.shape[0]
    width = qkv_raw.shape[2]
    heads = width // HEAD_DIM
    total = rows + HALO
    devices = lax.axis_size("seq")
    columns = lax.axis_size("head")
    piece = rows // columns
    share = devices // heads
    raw = qkv_raw.transpose(1, 0, 2)
    in_hbm = functools.partial(pltpu.with_memory_space_constraint, memory_space=pltpu.HBM)
    hd = HEAD_DIM


    smem = pl.BlockSpec(memory_space=pltpu.SMEM)
    params = pltpu.CompilerParams(vmem_limit_bytes=16 * 1024 * 1024)

    vmem = pl.BlockSpec(memory_space=pltpu.VMEM)
    hbm = pl.BlockSpec(memory_space=pltpu.HBM)
    dma = pltpu.SemaphoreType.DMA

    def flat_call(body, ins, outs, scratch, *args):
        spec = hbm if body is conv_kernel else smem
        return pl.pallas_call(
            body,
            in_specs=[spec] + ins,
            out_specs=[hbm if out.memory_space == pltpu.HBM else vmem for out in outs],
            out_shape=outs,
            scratch_shapes=scratch,
            compiler_params=params,
        )(in_hbm(doc_starts) if spec is hbm else doc_starts, *[in_hbm(a) if spec is hbm else a for a, spec in zip(args, ins)])

    wide = pltpu.VMEM((rows, width), bf16)
    tall = pltpu.VMEM((rows, width), f32)
    keys, values, message, rims, taps = flat_call(
        conv_kernel,
        [hbm] * 4,
        [
            wide, wide, pltpu.VMEM((devices // 2, 6 * SHARE, hd), bf16),
            pltpu.VMEM((7, HALO, width), bf16), pltpu.VMEM((4, TAPS, width), f32),
        ],
        [
            pltpu.VMEM((2, rows, width), bf16), pltpu.VMEM((1, width), f32),
            pltpu.SMEM(doc_starts.shape, jnp.int32), dma((8,)),
        ],
        raw, cotangent, conv_weight, norm_gain.reshape(1, width),
    )

    def swap(parts):
        return lax.all_to_all(parts, "seq", 0, 0, tiled=True)

    def scan(body, shape, parts, *others):
        (found,) = flat_call(
            functools.partial(body, rows), [vmem] * (1 + len(others)),
            [pltpu.VMEM(shape, bf16)], [], parts, *others,
        )
        return found

    beside = flat_call(
        local_kernel, [hbm] + [vmem] * 3, [wide, wide, wide, tall],
        [pltpu.VMEM((2, rows, width), bf16), dma((2,))],
        raw, taps, keys, values,
    )
    swapped = swap(message.reshape(devices, 3 * SHARE, hd)).reshape(message.shape)
    message, beside = lax.optimization_barrier((swapped, beside))
    queries, slope_q, slope_k, local = beside
    message = scan(forward_kernel, (devices, 2 * SHARE, hd), message, taps)
    incoming = swap(message)
    attn_out, grad_norm, back, top_qkv, top_slope = flat_call(
        norm_kernel,
        [vmem] * 10,
        [
            pltpu.VMEM((columns, piece, width), bf16), wide,
            pltpu.VMEM((heads * hd, hd), bf16), pltpu.VMEM((3, HALO, width), bf16),
            pltpu.VMEM((2, SHARE, width), f32),
        ],
        [],
        queries, local, incoming, cotangent, rims, taps, slope_q, slope_k, keys, values,
    )
    out_q, edge_qkv, edge_slope, local_k, local_v = flat_call(
        gradient_kernel,
        [vmem] * 10,
        [
            pltpu.VMEM((columns, piece, width), bf16), pltpu.VMEM((3, HALO, width), bf16),
            pltpu.VMEM((HALO, width), f32), pltpu.VMEM((total, width), bf16),
            pltpu.VMEM((total, width), bf16),
        ],
        [pltpu.VMEM((HALO, width), bf16)],
        queries, keys, values, top_qkv, top_slope, grad_norm, slope_q, incoming, rims, taps,
    )
    back = swap(back.reshape(devices, SHARE, hd))
    back, out_q, edge_qkv, edge_slope, local_k, local_v = lax.optimization_barrier(
        (back, out_q, edge_qkv, edge_slope, local_k, local_v)
    )
    pairs = (devices // 2, 2 * SHARE, hd)
    back = scan(backward_kernel, pairs, back.reshape(pairs))
    future = swap(back.reshape(devices, SHARE, hd))
    (sent,) = flat_call(
        last_kernel, [vmem] * 13, [pltpu.VMEM((columns, 4, piece, width), bf16)], [dma((2,))],
        keys, values, top_qkv, top_slope, edge_qkv, slope_k, edge_slope, local_k, local_v,
        future.reshape(heads * hd, hd), taps, attn_out, out_q,
    )
    sent = lax.all_to_all(sent, "head", 0, 0, tiled=True)
    out, grad = pl.pallas_call(
        gather_kernel,
        out_shape=[
            jax.ShapeDtypeStruct((piece, columns * width), bf16),
            jax.ShapeDtypeStruct((3, piece, columns * width), bf16),
        ],
        compiler_params=params,
    )(sent)
    return out, grad.transpose(1, 0, 2)


def solution(mesh):
    return jax.shard_map(
        shards,
        mesh=mesh,
        in_specs=(P("seq", None, "head"), P(None, None, "head"), P("head"), P(), P("seq", "head")),
        out_specs=(P(("seq", "head"), None), P(("seq", "head"), None, None)),
        check_vma=False,
    )
```
